512 devices in a mesh: gx: 16 (over x_lo, y, core), gy: 16 (over z), gz: 2 (over x_hi).
Axes of the slice: x: 4 (x_hi: 2, x_lo: 2; x = x_hi * 2 + x_lo), y: 4, z: 16, core: 2. Of those that a mesh axis runs over, the one named last changes fastest.
Arguments:
- thermal_anomaly: float32 [256, 256, 256], P('gx', 'gy', 'gz'), may hold values from -6 to 6
- specific_vapour: float32 [256, 256, 256], P('gx', 'gy', 'gz'), may hold values from -6 to 6
- server_thermal_load: float32 [256, 256, 256], P('gx', 'gy', 'gz'), may hold values from -5 to 5
- lateral_mixing_coefficient: float32 [256, 256, 256], P('gx', 'gy', 'gz'), may hold values from 40 to 800
- upward_mixing_coefficient: float32 [256, 256, 256], P('gx', 'gy', 'gz'), may hold values from 0.1 to 0.25
- cfl_along_lateral_axis: float32 [256, 256, 256], P('gx', 'gy', 'gz'), may hold values from -30 to 30
- cfl_across_lateral_axis: float32 [256, 256, 256], P('gx', 'gy', 'gz'), may hold values from -30 to 30
- cfl_upward_axis: float32 [256, 256, 256], P('gx', 'gy', 'gz'), may hold values from -0.15 to 0.15
Outputs:
- temperature_new: float32 [256, 256, 256], P('gx', 'gy', 'gz')
- humidity_new: float32 [256, 256, 256], P('gx', 'gy', 'gz')
The draws below stay inside these ranges and needn't reach their ends.
All inputs are finite; a program needn't handle non-finite values.
Results may differ from the reference program's by a relative error of at most 0.0003.
Values sent between devices are 32-bit elements; how exact they have to be, the bound alone decides.
A program may use at most 64 MiB of HBM per device.

```python
import math
import jax
import jax.numpy as jnp
from jax import lax

NX = 256
NY = 256
NZ = 256


def smooth_part(key):
    keys = jax.random.split(key, 3)
    phases = jax.random.uniform(keys[0], (4,), jnp.float32, 0.0, 6.2831853)
    amps = jax.random.uniform(keys[1], (4,), jnp.float32, 0.4, 0.8)
    first = (jnp.arange(NX, dtype=jnp.float32) * (6.2831853 / NX)).reshape(NX, 1, 1)
    second = (jnp.arange(NY, dtype=jnp.float32) * (6.2831853 / NY)).reshape(1, NY, 1)
    plane = amps[0] * jnp.sin(first + phases[0]) * jnp.cos(second + phases[1]) + amps[1] * jnp.sin(2.0 * first + phases[2]) + amps[2] * jnp.cos(2.0 * second + phases[3]) + amps[3] * jnp.sin(first + second + phases[1] - phases[2])
    column = jax.random.uniform(keys[2], (1, 1, NZ), jnp.float32, 0.5, 1.5)
    return plane * column


def field_normal(key):
    keys = jax.random.split(key, 2)
    rough = jax.random.normal(keys[0], (NX, NY, NZ), jnp.float32)
    return jnp.clip(0.8 * rough + smooth_part(keys[1]), -6.0, 6.0)


def draw_thermal_anomaly(key, part):
    inner = jax.random.fold_in(key, 11)
    return field_normal(inner)


def draw_specific_vapour(key, part):
    inner = jax.random.fold_in(key, 23)
    return field_normal(inner)


def draw_server_thermal_load(key, part):
    inner = jax.random.fold_in(key, 37)
    keys = jax.random.split(inner, 3)
    factor = jax.random.uniform(keys[0], (NX, NY, NZ), jnp.float32, 0.5, 1.5)
    rough = 0.25 * jax.random.normal(keys[1], (NX, NY, NZ), jnp.float32)
    smooth = smooth_part(keys[2])
    return jnp.clip(smooth * factor + rough, -5.0, 5.0)


def block_levels(own_key, dims, cuts, smallest, high):
    level = 1.0
    for dim, blocks in cuts:
        draws = jax.random.uniform(jax.random.fold_in(jax.random.fold_in(own_key, 6), dim), (blocks,), jnp.float32, smallest / len(cuts), high / len(cuts))
        level = level * jnp.repeat(jnp.exp(draws), dims[dim] // blocks).reshape((-1,) + (1,) * (len(dims) - 1 - dim))
    return level


def setup_inputs(seed: int = 0) -> dict:
    arg_keys = jax.random.split(jax.random.key(seed), 9)
    thermal_anomaly = draw_thermal_anomaly(jax.random.fold_in(arg_keys[8], 71), 0)
    specific_vapour = draw_specific_vapour(jax.random.fold_in(arg_keys[8], 71), 0)
    server_thermal_load = draw_server_thermal_load(jax.random.fold_in(arg_keys[8], 71), 0)
    lateral_mixing_coefficient = jnp.clip(jnp.exp(math.log(800.0) - 2.9957323 * jax.random.uniform(arg_keys[3], (NX, NY, NZ), jnp.float32) ** block_levels(arg_keys[3], (NX, NY, NZ), ((0, 16), (1, 16), (2, 2)), -0.2, 0.2)), 40.0, 800.0)
    upward_mixing_coefficient = jnp.clip(jnp.exp(math.log(0.25) - 0.9162907 * jax.random.uniform(arg_keys[4], (NX, NY, NZ), jnp.float32) ** block_levels(arg_keys[4], (NX, NY, NZ), ((0, 16), (1, 16), (2, 2)), -0.2, 0.2)), 0.1, 0.25)
    cfl_along_lateral_axis = jnp.clip(jax.random.uniform(arg_keys[5], (NX, NY, NZ), jnp.float32, -30.0, 30.0) * block_levels(arg_keys[5], (NX, NY, NZ), ((0, 16), (1, 16), (2, 2)), -0.4, 0.0), -30.0, 30.0)
    cfl_across_lateral_axis = jnp.clip(jax.random.uniform(arg_keys[6], (NX, NY, NZ), jnp.float32, -30.0, 30.0) * block_levels(arg_keys[6], (NX, NY, NZ), ((0, 16), (1, 16), (2, 2)), -0.4, 0.0), -30.0, 30.0)
    cfl_upward_axis = jnp.clip(jax.random.uniform(arg_keys[7], (NX, NY, NZ), jnp.float32, -0.15, 0.15) * block_levels(arg_keys[7], (NX, NY, NZ), ((0, 16), (1, 16), (2, 2)), -0.4, 0.0), -0.15, 0.15)
    return dict(thermal_anomaly=thermal_anomaly, specific_vapour=specific_vapour, server_thermal_load=server_thermal_load, lateral_mixing_coefficient=lateral_mixing_coefficient, upward_mixing_coefficient=upward_mixing_coefficient, cfl_along_lateral_axis=cfl_along_lateral_axis, cfl_across_lateral_axis=cfl_across_lateral_axis, cfl_upward_axis=cfl_upward_axis)


vapour_scaling = 0.8


def shifted_ahead(prior_tracer, position):
    length = prior_tracer.shape[position]
    inner = lax.slice_in_dim(prior_tracer, 1, length, axis=position)
    zeros = jnp.zeros_like(lax.slice_in_dim(prior_tracer, 0, 1, axis=position))
    return jnp.concatenate([inner, zeros], axis=position)


def shifted_behind(prior_tracer, position):
    length = prior_tracer.shape[position]
    inner = lax.slice_in_dim(prior_tracer, 0, length - 1, axis=position)
    zeros = jnp.zeros_like(lax.slice_in_dim(prior_tracer, 0, 1, axis=position))
    return jnp.concatenate([zeros, inner], axis=position)


def explicit(prior_tracer, east_coef, west_coef, position):
    ahead = shifted_ahead(prior_tracer, position) - prior_tracer
    behind = shifted_behind(prior_tracer, position) - prior_tracer
    return east_coef * ahead + west_coef * behind


def solve_lines(east_coef, west_coef, right_side):
    lower_band = -west_coef
    diagonal_band = 1.0 + east_coef + west_coef
    upper_band = -east_coef

    def forward(carried, cell_data):
        upper_before, right_before = carried
        lower_cell, diagonal_cell, upper_cell, right_cell = cell_data
        pivots = diagonal_cell - lower_cell * upper_before
        upper_now = upper_cell / pivots
        right_now = (right_cell - lower_cell * right_before) / pivots
        return (upper_now, right_now), (upper_now, right_now)

    start = (jnp.zeros_like(right_side[0]), jnp.zeros_like(right_side[0]))
    unused, ratios = lax.scan(forward, start, (lower_band, diagonal_band, upper_band, right_side))

    def backward(value_after, cell_data):
        upper_ratio, right_ratio = cell_data
        value = right_ratio - upper_ratio * value_after
        return value, value

    unused_end, values = lax.scan(backward, jnp.zeros_like(right_side[0]), ratios, reverse=True)
    return values


def reference(thermal_anomaly, specific_vapour, server_thermal_load, lateral_mixing_coefficient, upward_mixing_coefficient, cfl_along_lateral_axis, cfl_across_lateral_axis, cfl_upward_axis):
    results = []
    for scaling_element, prior_tracer, coefficient_element in ((1.0, thermal_anomaly, 1.0), (vapour_scaling, specific_vapour, 0.0)):
        east_x = scaling_element * lateral_mixing_coefficient - 0.5 * cfl_along_lateral_axis
        west_x = scaling_element * lateral_mixing_coefficient + 0.5 * cfl_along_lateral_axis
        east_y = scaling_element * lateral_mixing_coefficient - 0.5 * cfl_across_lateral_axis
        west_y = scaling_element * lateral_mixing_coefficient + 0.5 * cfl_across_lateral_axis
        east_z = scaling_element * upward_mixing_coefficient - 0.5 * cfl_upward_axis
        west_z = scaling_element * upward_mixing_coefficient + 0.5 * cfl_upward_axis
        source = coefficient_element * server_thermal_load
        first_side = prior_tracer + explicit(prior_tracer, east_y, west_y, 1) + explicit(prior_tracer, east_z, west_z, 2) + source
        half_field = solve_lines(east_x, west_x, first_side)
        second_side = half_field + explicit(half_field, east_x, west_x, 0) + explicit(half_field, east_z, west_z, 2) + source
        moved = solve_lines(jnp.moveaxis(east_y, 1, 0), jnp.moveaxis(west_y, 1, 0), jnp.moveaxis(second_side, 1, 0))
        results.append(jnp.moveaxis(moved, 0, 1))
    return (results[0], results[1])
```

```python
import functools

import jax
import jax.numpy as jnp
from jax import lax
from jax.experimental import pallas as pl
from jax.experimental.pallas import tpu as pltpu
from jax.sharding import PartitionSpec as P

vapour_scaling = 0.8
N = 16
LANES = 128
SOLVERS = 4
MESH = pl.DeviceIdType.MESH
F32 = jnp.float32


def kernel(
    t_in, h_in, load_in, k_in, kz_in, cx_in, cy_in, cz_in,
    t_out, h_out,
    fields, load, mix, mix_z, cfl_x, cfl_y, cfl_z, result,
    side, mask_z, half,
    first_w, last_w, inv, wi, ratio_c, from_left, from_right, part,
    tmp_a, tmp_b,
    y_send, y_face, z_send, z_face,
    coef_send, coef_recv, side_send, side_recv, back_send, back_recv, lu,
    in_sem, out_sem, y_sem, z_sem, net_sem,
):
    gx, gy, gz = lax.axis_index("gx"), lax.axis_index("gy"), lax.axis_index("gz")
    core = lax.rem(gx, 2)

    tile_x = lax.rem(lax.div(gx, 2), 4)
    tile_y = lax.div(gy, 4)
    axes = (
        dict(
            me=gx, tile=tile_x, solves=gx == 8 * lax.rem(tile_x, 2) + 2 * tile_x,
            solver=lambda s: 8 * (s % 2) + 2 * s, device=lambda i: (i, gy, gz),
        ),
        dict(
            me=gy, tile=tile_y, solves=gy == 4 * tile_y + 2 * core,
            solver=lambda s: 4 * s + 2 * core, device=lambda i: (gx, i, gz),
        ),
    )

    barrier = pltpu.get_barrier_semaphore()

    def greet(device):
        pl.semaphore_signal(barrier, inc=1, device_id=device, device_id_type=MESH)

    greet((gx, gy, 1 - gz))
    expected = 1
    pl.when(gy > 0)(lambda: greet((gx, gy - 1, gz)))
    pl.when(gy < N - 1)(lambda: greet((gx, gy + 1, gz)))
    expected += jnp.where(gy > 0, 1, 0) + jnp.where(gy < N - 1, 1, 0)
    for ax in axes:
        for s in range(SOLVERS):
            pl.when(ax["me"] != ax["solver"](s))(
                functools.partial(greet, ax["device"](ax["solver"](s)))
            )

        @pl.when(ax["solves"])
        def _(ax=ax):
            @pl.loop(0, N)
            def _(i):
                pl.when(i != ax["me"])(lambda: greet(ax["device"](i)))

        expected += jnp.where(ax["solves"], N - 1 + SOLVERS - 1, SOLVERS)

    loads = [
        pltpu.make_async_copy(src, dst, in_sem.at[n])
        for n, (src, dst) in enumerate((
            (t_in, fields.at[0]), (h_in, fields.at[1]), (k_in, mix), (cx_in, cfl_x),
            (cy_in, cfl_y), (kz_in, mix_z), (cz_in, cfl_z), (load_in, load),
        ))
    ]
    for copy in loads:
        copy.start()

    lane = lax.broadcasted_iota(jnp.int32, (2, N, LANES), 2)
    field = lax.broadcasted_iota(jnp.int32, (2, N, LANES), 0)
    ratio = jnp.where(field == 0, 1.0, vapour_scaling).astype(F32)
    weight = jnp.where(field == 0, 1.0, 0.0).astype(F32)
    lane2 = lax.broadcasted_iota(jnp.int32, (N, LANES), 1)
    face = jnp.where(gz == 0, LANES - 1, 0)

    def along(n):
        return pl.ds(N * n, N)

    def across(n):
        return pl.ds(n, N, stride=N)

    def pair(ref, rows):
        return jnp.broadcast_to(ref[rows, :][None], (2, N, LANES))

    def pack_column(rows, y, packed):
        for f in range(2):
            n = 1 + N * f + y
            moved = pltpu.roll(rows[f], n + 1 - gz, 1)
            packed = jnp.where(lane2 == n, moved, packed)
        return packed

    def unpack_column(packed, y):
        return jnp.stack(
            [pltpu.roll(packed, LANES - 1 - (1 + N * f + y) + gz, 1) for f in range(2)]
        )

    loads[0].wait()
    loads[1].wait()
    y_send[0] = fields[:, across(0), :]
    y_send[1] = fields[:, across(N - 1), :]
    packed = jnp.zeros((N, LANES), F32)
    for y in range(N):
        packed = pack_column(fields[:, across(y), :], y, packed)
    z_send[0] = packed
    pl.when(gy == 0)(lambda: y_face.__setitem__(0, jnp.zeros((2, N, LANES), F32)))
    pl.when(gy == N - 1)(lambda: y_face.__setitem__(1, jnp.zeros((2, N, LANES), F32)))

    def factor(d, rows, cfl):
        def bands(k):
            mixed = ratio * pair(mix, rows(k))
            speed = 0.5 * pair(cfl, rows(k))
            return mixed - speed, mixed + speed

        rest, chain = None, None
        for k in range(N):
            east, west = bands(k)
            v = 1.0 + (west if rest is None else west * rest)
            i = 1.0 / (v + east)
            c = east * i
            rest = v * i
            w = west * i
            chain = w if chain is None else w * chain
            inv[d, k] = i
            wi[d, k] = w
            ratio_c[d, k] = c
            tmp_a[k] = chain
        q, t, prod = chain, c, None
        from_left[d, N - 1] = q
        from_right[d, N - 1] = t
        ends = [None, None, q, t]
        for k in range(N - 1, -1, -1):
            if k < N - 1:
                c = ratio_c[d, k]
                q = tmp_a[k] + c * q
                t = c * t
                from_left[d, k] = q
                from_right[d, k] = t
        ends[0], ends[1] = q, t
        for v, value in enumerate(ends):
            for s in range(SOLVERS):
                coef_send[d, s, v] = value[s // 2, 8 * (s % 2) : 8 * (s % 2) + 8]

    def weights(d, rows, cfl):
        def bands(k):
            mixed = ratio * pair(mix, rows(k))
            speed = 0.5 * pair(cfl, rows(k))
            return mixed - speed, mixed + speed

        rest, prod = None, None
        for k in range(N - 1, -1, -1):
            east, west = bands(k)
            v = 1.0 + (east if rest is None else east * rest)
            i = 1.0 / (v + west)
            rest = v * i
            tmp_a[k] = i
            tmp_b[k] = east * i
            last_w[d, k] = inv[d, k] if prod is None else inv[d, k] * prod
            prod = wi[d, k] if prod is None else wi[d, k] * prod
        prod = None
        for k in range(N):
            first_w[d, k] = tmp_a[k] if prod is None else tmp_a[k] * prod
            prod = tmp_b[k] if prod is None else tmp_b[k] * prod

    def to_solvers(d, send, recv, kind):
        ax = axes[d]
        for s in range(SOLVERS):
            copy = pltpu.make_async_remote_copy(
                send.at[d, s], recv.at[d, ax["me"]], net_sem.at[d, kind, 0], net_sem.at[d, kind, 1],
                device_id=ax["device"](ax["solver"](s)), device_id_type=MESH,
            )
            pl.when(ax["me"] != ax["solver"](s))(copy.start)

            @pl.when(ax["me"] == ax["solver"](s))
            def _():
                recv[d, ax["me"]] = send[d, s]

    def wait_slots(ref, count, sem):
        pltpu.make_async_copy(ref.at[pl.ds(0, count)], ref.at[pl.ds(0, count)], sem).wait()

    def sent_to_solvers(d, send, kind):
        pl.when(axes[d]["solves"])(
            lambda: wait_slots(send.at[d], SOLVERS - 1, net_sem.at[d, kind, 0])
        )
        pl.when(jnp.logical_not(axes[d]["solves"]))(
            lambda: wait_slots(send.at[d], SOLVERS, net_sem.at[d, kind, 0])
        )

    def solver_factor(d):
        @pl.when(axes[d]["solves"])
        def _():
            wait_slots(coef_recv.at[d], N - 1, net_sem.at[d, 0, 1])
            beta = None
            for i in range(N):
                q0, t0, q1, t1 = (coef_recv[d, i, v] for v in range(4))
                if beta is None:
                    dinv = jnp.ones_like(q0)
                    b = jnp.zeros_like(q0)
                    tau = t0
                    beta = t1
                    a = b
                    dq = b
                else:
                    dinv = 1.0 / (1.0 - q0 * beta)
                    b = q1 * beta * dinv
                    tau = t0 * dinv
                    beta = t1 + b * t0
                    a = q1 + b * q0
                    dq = dinv * q0
                for n, value in enumerate((dinv, dq, a, b, tau, beta)):
                    lu[d, i, n] = value

    def solver_solve(d):
        ax = axes[d]

        @pl.when(ax["solves"])
        def _():
            wait_slots(side_recv.at[d], N - 1, net_sem.at[d, 1, 1])
            alpha, alphas, phis = None, [], []
            for i in range(N):
                p0, p1 = side_recv[d, i, 0], side_recv[d, i, 1]
                if alpha is None:
                    phi, alpha = p0, p1
                else:
                    phi = lu[d, i, 0] * p0 + lu[d, i, 1] * alpha
                    alpha = (p1 + lu[d, i, 3] * p0) + lu[d, i, 2] * alpha
                alphas.append(alpha)
                phis.append(phi)
            zero = jnp.zeros((8, LANES), F32)
            first, firsts, lasts = zero, [None] * N, [None] * N
            for i in range(N - 1, -1, -1):
                lasts[i] = alphas[i] + lu[d, i, 5] * first
                first = phis[i] + lu[d, i, 4] * first
                firsts[i] = first
            for i in range(N):
                back_send[d, i, 0] = lasts[i - 1] if i > 0 else zero
                back_send[d, i, 1] = firsts[i + 1] if i < N - 1 else zero

            @pl.loop(0, N)
            def _(i):
                copy = pltpu.make_async_remote_copy(
                    back_send.at[d, i], back_recv.at[d, ax["tile"]],
                    net_sem.at[d, 2, 0], net_sem.at[d, 2, 1],
                    device_id=ax["device"](i), device_id_type=MESH,
                )
                pl.when(i != ax["me"])(copy.start)

            back_recv[d, ax["tile"]] = back_send[d, ax["me"]]

    def wait_back(d):
        pl.when(axes[d]["solves"])(
            lambda: wait_slots(back_recv.at[d], SOLVERS - 1, net_sem.at[d, 2, 1])
        )
        pl.when(jnp.logical_not(axes[d]["solves"]))(
            lambda: wait_slots(back_recv.at[d], SOLVERS, net_sem.at[d, 2, 1])
        )
        return tuple(
            back_recv[d, :, v].reshape(2, N, LANES) for v in range(2)
        )

    def ends_of(d, rhs):
        sums = [None, None]
        for k in range(N):
            b = rhs(k)
            terms = first_w[d, k] * b, last_w[d, k] * b
            sums = [x if s is None else s + x for s, x in zip(sums, terms)]
        for v in range(2):
            for s in range(SOLVERS):
                side_send[d, s, v] = sums[v][s // 2, 8 * (s % 2) : 8 * (s % 2) + 8]

    def particular(d, rhs):
        g = None
        for k in range(N):
            g = inv[d, k] * rhs(k) + (0.0 if g is None else wi[d, k] * g)
            tmp_a[k] = g
        value = g
        part[d, N - 1] = value
        for k in range(N - 2, -1, -1):
            value = tmp_a[k] + ratio_c[d, k] * value
            part[d, k] = value

    loads[2].wait()
    loads[3].wait()
    factor(0, along, cfl_x)

    pl.semaphore_wait(barrier, expected)

    z_copy = [
        pltpu.make_async_remote_copy(
            z_send.at[n], z_face.at[n], z_sem.at[n, 0], z_sem.at[n, 1],
            device_id=(gx, gy, 1 - gz), device_id_type=MESH,
        )
        for n in range(2)
    ]
    y_up = pltpu.make_async_remote_copy(
        y_send.at[1], y_face.at[0], y_sem.at[0, 0], y_sem.at[0, 1],
        device_id=(gx, gy + 1, gz), device_id_type=MESH,
    )
    y_down = pltpu.make_async_remote_copy(
        y_send.at[0], y_face.at[1], y_sem.at[1, 0], y_sem.at[1, 1],
        device_id=(gx, gy - 1, gz), device_id_type=MESH,
    )
    z_copy[0].start()
    pl.when(gy < N - 1)(y_up.start)
    pl.when(gy > 0)(y_down.start)
    to_solvers(0, coef_send, coef_recv, 0)

    weights(0, along, cfl_x)

    for n in range(4, 8):
        loads[n].wait()
    toward = jnp.where(gz == 0, -0.5, 0.5).astype(F32)

    def vertical(v, y):
        mixed = ratio * pair(mix_z, across(y))
        cfl = pair(cfl_z, across(y))
        up = jnp.where(lane == LANES - 1, 0.0, pltpu.roll(v, LANES - 1, 2))
        down = jnp.where(lane == 0, 0.0, pltpu.roll(v, 1, 2))
        return (mixed - 0.5 * cfl) * (up - v) + (mixed + 0.5 * cfl) * (down - v)

    edge_coef = [None, None]
    for y in range(N):
        here = fields[:, across(y), :]
        mixed = ratio * pair(mix, across(y))
        speed = 0.5 * pair(cfl_y, across(y))
        east, west = mixed - speed, mixed + speed
        ahead = fields[:, across(y + 1), :] - here if y < N - 1 else -here
        behind = fields[:, across(y - 1), :] - here if y > 0 else -here
        value = here + (east * ahead + west * behind) + vertical(here, y)
        value = value + weight * pair(load, across(y))
        side[:, along(y), :] = value
        outward = ratio * pair(mix_z, across(y)) + toward * pair(cfl_z, across(y))
        mask_z[y] = jnp.where(lane == face, outward, 0.0)
        if y == 0:
            edge_coef[0] = west
        if y == N - 1:
            edge_coef[1] = east

    factor(1, across, cfl_y)
    to_solvers(1, coef_send, coef_recv, 0)
    weights(1, across, cfl_y)

    z_copy[0].wait_recv()
    pl.when(gy > 0)(y_up.wait_recv)
    pl.when(gy < N - 1)(y_down.wait_recv)
    got = z_face[0]
    for y in range(N):
        value = side[:, along(y), :] + mask_z[y] * unpack_column(got, y)
        if y == 0:
            value = value + edge_coef[0] * y_face[0]
        if y == N - 1:
            value = value + edge_coef[1] * y_face[1]
        side[:, along(y), :] = value

    def first_rhs(k):
        return side[:, across(k), :]

    ends_of(0, first_rhs)
    to_solvers(0, side_send, side_recv, 1)
    solver_factor(0)
    solver_solve(0)
    particular(0, first_rhs)
    left, right = wait_back(0)
    for k in range(N):
        half[:, along(k), :] = part[0, k] + from_left[0, k] * left + from_right[0, k] * right

    packed = jnp.zeros((N, LANES), F32)
    for y in range(N):
        packed = pack_column(half[:, across(y), :], y, packed)
    z_send[1] = packed
    z_copy[1].start()
    for y in range(N):
        here = half[:, across(y), :]
        value = 2.0 * here - side[:, along(y), :] + vertical(here, y)
        side[:, along(y), :] = value + weight * pair(load, across(y))
    solver_factor(1)
    z_copy[1].wait_recv()
    got = z_face[1]
    for y in range(N):
        side[:, along(y), :] = side[:, along(y), :] + mask_z[y] * unpack_column(got, y)

    def second_rhs(k):
        return side[:, along(k), :]

    ends_of(1, second_rhs)
    to_solvers(1, side_send, side_recv, 1)
    solver_solve(1)
    particular(1, second_rhs)
    left, right = wait_back(1)
    for k in range(N):
        result[:, across(k), :] = part[1, k] + from_left[1, k] * left + from_right[1, k] * right
    outs = [
        pltpu.make_async_copy(result.at[f], out, out_sem.at[f]) for f, out in enumerate((t_out, h_out))
    ]
    for copy in outs:
        copy.start()

    for n in range(2):
        z_copy[n].wait_send()
    pl.when(gy < N - 1)(y_up.wait_send)
    pl.when(gy > 0)(y_down.wait_send)
    for d in range(2):
        sent_to_solvers(d, coef_send, 0)
        sent_to_solvers(d, side_send, 1)
        pl.when(axes[d]["solves"])(
            lambda d=d: wait_slots(back_send.at[d], N - 1, net_sem.at[d, 2, 0])
        )
    for copy in outs:
        copy.wait()


def body(*args):
    flat = [a.reshape(N * N, LANES) for a in args]
    block = (N * N, LANES)
    rows = (N, 2, N, LANES)
    both = (2, N, 2, N, LANES)
    vmem = lambda *shape: pltpu.VMEM(shape, F32)
    outs = pl.pallas_call(
        kernel,
        out_shape=[jax.ShapeDtypeStruct(block, F32)] * 2,
        in_specs=[pl.BlockSpec(memory_space=pl.ANY)] * 8,
        out_specs=[pl.BlockSpec(memory_space=pl.ANY)] * 2,
        scratch_shapes=[
            vmem(2, *block),
            *[vmem(*block)] * 6,
            vmem(2, *block),
            vmem(2, *block), vmem(*rows), vmem(2, *block),
            *[vmem(*both)] * 8,
            vmem(*rows), vmem(*rows),
            vmem(2, 2, N, LANES), vmem(2, 2, N, LANES),
            vmem(2, N, LANES), vmem(2, N, LANES),
            vmem(2, SOLVERS, 4, 8, LANES), vmem(2, N, 4, 8, LANES),
            vmem(2, SOLVERS, 2, 8, LANES), vmem(2, N, 2, 8, LANES),
            vmem(2, N, 2, 8, LANES), vmem(2, SOLVERS, 2, 8, LANES),
            vmem(2, N, 6, 8, LANES),
            pltpu.SemaphoreType.DMA((8,)), pltpu.SemaphoreType.DMA((2,)),
            pltpu.SemaphoreType.DMA((2, 2)), pltpu.SemaphoreType.DMA((2, 2)),
            pltpu.SemaphoreType.DMA((2, 3, 2)),
        ],
        compiler_params=pltpu.CompilerParams(
            collective_id=0, has_side_effects=True, vmem_limit_bytes=32 * 1024 * 1024
        ),
    )(*flat)
    return tuple(o.reshape(N, N, LANES) for o in outs)


def solution(mesh):
    spec = P("gx", "gy", "gz")
    return jax.shard_map(
        body, mesh=mesh, in_specs=(spec,) * 8, out_specs=(spec,) * 2, check_vma=False
    )
```

```python
import functools

import jax
import jax.numpy as jnp
from jax import lax
from jax.experimental import pallas as pl
from jax.experimental.pallas import tpu as pltpu
from jax.sharding import PartitionSpec as P

vapour_scaling = 0.8
N = 16
LANES = 128
SOLVERS = 4
MESH = pl.DeviceIdType.MESH
F32 = jnp.float32


def kernel(
    t_in, h_in, load_in, k_in, kz_in, cx_in, cy_in, cz_in,
    t_out, h_out,
    fields, load, mix, mix_z, cfl_x, cfl_y, cfl_z,
    side, mask_z, half,
    first_w, last_w, inv, wi, ratio_c, from_left, from_right, part,
    tmp_a, tmp_b,
    y_send, y_face, z_send, z_face,
    coef_send, coef_recv, side_send, side_recv, back_send, back_recv, lu,
    in_sem, y_sem, z_sem, net_sem, far_sem,
):
    gx, gy, gz = lax.axis_index("gx"), lax.axis_index("gy"), lax.axis_index("gz")
    core = lax.rem(gx, 2)

    tile_x = lax.rem(lax.div(gx, 2), 4)
    tile_y = lax.rem(lax.div(gy, 2), 4)
    axes = (
        dict(
            me=gx, tile=tile_x, solves=gx == 8 * lax.rem(tile_x, 2) + 2 * tile_x,
            solvers=lambda s: (8 * (s % 2) + 2 * s,), device=lambda i: (i, gy, gz),
            served=N, serve=lambda i: i,
        ),
        dict(
            me=gy, tile=tile_y, solves=lax.rem(gy, 2) == core,
            solvers=lambda s: (2 * s + core, N // 2 + 2 * s + core), device=lambda i: (gx, i, gz),
            served=N // 2, serve=lambda i: lax.rem(gy + N - N // 4 + i, N),
        ),
    )

    loads = [
        pltpu.make_async_copy(src, dst, in_sem.at[n])
        for n, (src, dst) in enumerate((
            (k_in, mix), (cx_in, cfl_x), (t_in, fields.at[0]), (h_in, fields.at[1]),
            (cy_in, cfl_y), (kz_in, mix_z), (cz_in, cfl_z), (load_in, load),
        ))
    ]
    for copy in loads:
        copy.start()

    def ring(step):
        return (gx, lax.rem(gy + step + N, N), gz)

    def signal(sem, device):
        pl.semaphore_signal(sem, inc=1, device_id=device, device_id_type=MESH)

    barrier = pltpu.get_barrier_semaphore()
    signal(barrier, (gx, gy, 1 - gz))
    signal(barrier, ring(1))
    signal(barrier, ring(-1))
    for s in range(SOLVERS):
        (solver,) = axes[0]["solvers"](s)
        pl.when(gx != solver)(functools.partial(signal, barrier, axes[0]["device"](solver)))

    @pl.when(axes[0]["solves"])
    def _():
        @pl.loop(0, N)
        def _(i):
            pl.when(i != gx)(lambda: signal(barrier, axes[0]["device"](i)))

    expected = 3 + jnp.where(axes[0]["solves"], N - 1 + SOLVERS - 1, SOLVERS)

    def tell(r):
        signal(far_sem.at[r], ring(1 << r))
        signal(far_sem.at[r], ring(-(1 << r)))

    def hear(r):
        pl.semaphore_wait(far_sem.at[r], 2)

    lane = lax.broadcasted_iota(jnp.int32, (2, N, LANES), 2)
    field = lax.broadcasted_iota(jnp.int32, (2, N, LANES), 0)
    ratio = jnp.where(field == 0, 1.0, vapour_scaling).astype(F32)
    weight = jnp.where(field == 0, 1.0, 0.0).astype(F32)
    lane2 = lax.broadcasted_iota(jnp.int32, (N, LANES), 1)
    face = jnp.where(gz == 0, LANES - 1, 0)

    def along(n):
        return pl.ds(N * n, N)

    def across(n):
        return pl.ds(n, N, stride=N)

    def pair(ref, rows):
        return jnp.broadcast_to(ref[rows, :][None], (2, N, LANES))

    def pack_column(rows, y, packed):
        for f in range(2):
            n = 1 + N * f + y
            moved = pltpu.roll(rows[f], n + 1 - gz, 1)
            packed = jnp.where(lane2 == n, moved, packed)
        return packed

    def unpack_column(packed, y):
        return jnp.stack(
            [pltpu.roll(packed, LANES - 1 - (1 + N * f + y) + gz, 1) for f in range(2)]
        )

    def factor(d, rows, cfl):
        def bands(k):
            mixed = ratio * pair(mix, rows(k))
            speed = 0.5 * pair(cfl, rows(k))
            return mixed - speed, mixed + speed

        rest, chain = None, None
        for k in range(N):
            east, west = bands(k)
            v = 1.0 + (west if rest is None else west * rest)
            i = 1.0 / (v + east)
            c = east * i
            rest = v * i
            w = west * i
            chain = w if chain is None else w * chain
            inv[d, k] = i
            wi[d, k] = w
            ratio_c[d, k] = c
            tmp_a[k] = chain
        q, t, prod = chain, c, None
        from_left[d, N - 1] = q
        from_right[d, N - 1] = t
        ends = [None, None, q, t]
        for k in range(N - 1, -1, -1):
            if k < N - 1:
                c = ratio_c[d, k]
                q = tmp_a[k] + c * q
                t = c * t
                from_left[d, k] = q
                from_right[d, k] = t
        ends[0], ends[1] = q, t
        for v, value in enumerate(ends):
            for s in range(SOLVERS):
                coef_send[d, s, v] = value[s // 2, 8 * (s % 2) : 8 * (s % 2) + 8]

    def weights(d, rows, cfl):
        def bands(k):
            mixed = ratio * pair(mix, rows(k))
            speed = 0.5 * pair(cfl, rows(k))
            return mixed - speed, mixed + speed

        rest, prod = None, None
        for k in range(N - 1, -1, -1):
            east, west = bands(k)
            v = 1.0 + (east if rest is None else east * rest)
            i = 1.0 / (v + west)
            rest = v * i
            tmp_a[k] = i
            tmp_b[k] = east * i
            last_w[d, k] = inv[d, k] if prod is None else inv[d, k] * prod
            prod = wi[d, k] if prod is None else wi[d, k] * prod
        prod = None
        for k in range(N):
            first_w[d, k] = tmp_a[k] if prod is None else tmp_a[k] * prod
            prod = tmp_b[k] if prod is None else tmp_b[k] * prod

    def to_solvers(d, send, recv, kind):
        ax = axes[d]
        for s in range(SOLVERS):
            for solver in ax["solvers"](s):
                copy = pltpu.make_async_remote_copy(
                    send.at[d, s], recv.at[d, ax["me"]],
                    net_sem.at[d, kind, 0], net_sem.at[d, kind, 1],
                    device_id=ax["device"](solver), device_id_type=MESH,
                )
                pl.when(ax["me"] != solver)(copy.start)

                @pl.when(ax["me"] == solver)
                def _():
                    recv[d, ax["me"]] = send[d, s]

    def wait_slots(ref, count, sem):
        pltpu.make_async_copy(ref.at[pl.ds(0, count)], ref.at[pl.ds(0, count)], sem).wait()

    def sent_to_solvers(d, send, kind):
        for _ in axes[d]["solvers"](0)[1:]:
            wait_slots(send.at[d], SOLVERS, net_sem.at[d, kind, 0])
        pl.when(axes[d]["solves"])(
            lambda: wait_slots(send.at[d], SOLVERS - 1, net_sem.at[d, kind, 0])
        )
        pl.when(jnp.logical_not(axes[d]["solves"]))(
            lambda: wait_slots(send.at[d], SOLVERS, net_sem.at[d, kind, 0])
        )

    def solver_factor(d):
        @pl.when(axes[d]["solves"])
        def _():
            wait_slots(coef_recv.at[d], N - 1, net_sem.at[d, 0, 1])
            beta = None
            for i in range(N):
                q0, t0, q1, t1 = (coef_recv[d, i, v] for v in range(4))
                if beta is None:
                    dinv = jnp.ones_like(q0)
                    b = jnp.zeros_like(q0)
                    tau = t0
                    beta = t1
                    a = b
                    dq = b
                else:
                    dinv = 1.0 / (1.0 - q0 * beta)
                    b = q1 * beta * dinv
                    tau = t0 * dinv
                    beta = t1 + b * t0
                    a = q1 + b * q0
                    dq = dinv * q0
                for n, value in enumerate((dinv, dq, a, b, tau, beta)):
                    lu[d, i, n] = value

    def solver_solve(d):
        ax = axes[d]

        @pl.when(ax["solves"])
        def _():
            wait_slots(side_recv.at[d], N - 1, net_sem.at[d, 1, 1])
            alpha, alphas, phis = None, [], []
            for i in range(N):
                p0, p1 = side_recv[d, i, 0], side_recv[d, i, 1]
                if alpha is None:
                    phi, alpha = p0, p1
                else:
                    phi = lu[d, i, 0] * p0 + lu[d, i, 1] * alpha
                    alpha = (p1 + lu[d, i, 3] * p0) + lu[d, i, 2] * alpha
                alphas.append(alpha)
                phis.append(phi)
            zero = jnp.zeros((8, LANES), F32)
            first, firsts, lasts = zero, [None] * N, [None] * N
            for i in range(N - 1, -1, -1):
                lasts[i] = alphas[i] + lu[d, i, 5] * first
                first = phis[i] + lu[d, i, 4] * first
                firsts[i] = first
            for i in range(N):
                back_send[d, i, 0] = lasts[i - 1] if i > 0 else zero
                back_send[d, i, 1] = firsts[i + 1] if i < N - 1 else zero

            @pl.loop(0, ax["served"])
            def _(i):
                j = ax["serve"](i)
                copy = pltpu.make_async_remote_copy(
                    back_send.at[d, j], back_recv.at[d, ax["tile"]],
                    net_sem.at[d, 2, 0], net_sem.at[d, 2, 1],
                    device_id=ax["device"](j), device_id_type=MESH,
                )
                pl.when(j != ax["me"])(copy.start)

            back_recv[d, ax["tile"]] = back_send[d, ax["me"]]

    def wait_back(d):
        pl.when(axes[d]["solves"])(
            lambda: wait_slots(back_recv.at[d], SOLVERS - 1, net_sem.at[d, 2, 1])
        )
        pl.when(jnp.logical_not(axes[d]["solves"]))(
            lambda: wait_slots(back_recv.at[d], SOLVERS, net_sem.at[d, 2, 1])
        )
        return tuple(
            back_recv[d, :, v].reshape(2, N, LANES) for v in range(2)
        )

    def ends_of(d, rhs):
        sums = [None, None]
        for k in range(N):
            b = rhs(k)
            terms = first_w[d, k] * b, last_w[d, k] * b
            sums = [x if s is None else s + x for s, x in zip(sums, terms)]
        for v in range(2):
            for s in range(SOLVERS):
                side_send[d, s, v] = sums[v][s // 2, 8 * (s % 2) : 8 * (s % 2) + 8]

    def particular(d, rhs):
        g = None
        for k in range(N):
            g = inv[d, k] * rhs(k) + (0.0 if g is None else wi[d, k] * g)
            tmp_a[k] = g
        value = g
        part[d, N - 1] = value
        for k in range(N - 2, -1, -1):
            value = tmp_a[k] + ratio_c[d, k] * value
            part[d, k] = value

    loads[0].wait()
    loads[1].wait()
    factor(0, along, cfl_x)

    loads[2].wait()
    loads[3].wait()
    y_send[0] = fields[:, across(0), :]
    y_send[1] = fields[:, across(N - 1), :]
    packed = jnp.zeros((N, LANES), F32)
    for y in range(N):
        packed = pack_column(fields[:, across(y), :], y, packed)
    z_send[0] = packed
    pl.when(gy == 0)(lambda: y_face.__setitem__(0, jnp.zeros((2, N, LANES), F32)))
    pl.when(gy == N - 1)(lambda: y_face.__setitem__(1, jnp.zeros((2, N, LANES), F32)))

    pl.semaphore_wait(barrier, expected)

    z_copy = [
        pltpu.make_async_remote_copy(
            z_send.at[n], z_face.at[n], z_sem.at[n, 0], z_sem.at[n, 1],
            device_id=(gx, gy, 1 - gz), device_id_type=MESH,
        )
        for n in range(2)
    ]
    y_up = pltpu.make_async_remote_copy(
        y_send.at[1], y_face.at[0], y_sem.at[0, 0], y_sem.at[0, 1],
        device_id=(gx, gy + 1, gz), device_id_type=MESH,
    )
    y_down = pltpu.make_async_remote_copy(
        y_send.at[0], y_face.at[1], y_sem.at[1, 0], y_sem.at[1, 1],
        device_id=(gx, gy - 1, gz), device_id_type=MESH,
    )
    z_copy[0].start()
    pl.when(gy < N - 1)(y_up.start)
    pl.when(gy > 0)(y_down.start)
    to_solvers(0, coef_send, coef_recv, 0)
    tell(0)

    weights(0, along, cfl_x)

    for n in range(4, 8):
        loads[n].wait()
    toward = jnp.where(gz == 0, -0.5, 0.5).astype(F32)

    def vertical(v, y):
        mixed = ratio * pair(mix_z, across(y))
        cfl = pair(cfl_z, across(y))
        up = jnp.where(lane == LANES - 1, 0.0, pltpu.roll(v, LANES - 1, 2))
        down = jnp.where(lane == 0, 0.0, pltpu.roll(v, 1, 2))
        return (mixed - 0.5 * cfl) * (up - v) + (mixed + 0.5 * cfl) * (down - v)

    edge_coef = [None, None]
    for y in range(N):
        here = fields[:, across(y), :]
        mixed = ratio * pair(mix, across(y))
        speed = 0.5 * pair(cfl_y, across(y))
        east, west = mixed - speed, mixed + speed
        ahead = fields[:, across(y + 1), :] - here if y < N - 1 else -here
        behind = fields[:, across(y - 1), :] - here if y > 0 else -here
        value = here + (east * ahead + west * behind) + vertical(here, y)
        value = value + weight * pair(load, across(y))
        side[:, along(y), :] = value
        outward = ratio * pair(mix_z, across(y)) + toward * pair(cfl_z, across(y))
        mask_z[y] = jnp.where(lane == face, outward, 0.0)
        if y == 0:
            edge_coef[0] = west
        if y == N - 1:
            edge_coef[1] = east

    factor(1, across, cfl_y)
    weights(1, across, cfl_y)
    hear(0)
    tell(1)

    z_copy[0].wait_recv()
    pl.when(gy > 0)(y_up.wait_recv)
    pl.when(gy < N - 1)(y_down.wait_recv)
    got = z_face[0]
    for y in range(N):
        value = side[:, along(y), :] + mask_z[y] * unpack_column(got, y)
        if y == 0:
            value = value + edge_coef[0] * y_face[0]
        if y == N - 1:
            value = value + edge_coef[1] * y_face[1]
        side[:, along(y), :] = value

    def first_rhs(k):
        return side[:, across(k), :]

    ends_of(0, first_rhs)
    to_solvers(0, side_send, side_recv, 1)
    hear(1)
    tell(2)
    solver_factor(0)
    solver_solve(0)
    particular(0, first_rhs)
    hear(2)
    to_solvers(1, coef_send, coef_recv, 0)
    left, right = wait_back(0)
    for k in range(N):
        half[:, along(k), :] = part[0, k] + from_left[0, k] * left + from_right[0, k] * right

    packed = jnp.zeros((N, LANES), F32)
    for y in range(N):
        packed = pack_column(half[:, across(y), :], y, packed)
    z_send[1] = packed
    z_copy[1].start()
    for y in range(N):
        here = half[:, across(y), :]
        value = 2.0 * here - side[:, along(y), :] + vertical(here, y)
        side[:, along(y), :] = value + weight * pair(load, across(y))
    z_copy[1].wait_recv()
    got = z_face[1]
    for y in range(N):
        side[:, along(y), :] = side[:, along(y), :] + mask_z[y] * unpack_column(got, y)

    def second_rhs(k):
        return side[:, along(k), :]

    ends_of(1, second_rhs)
    to_solvers(1, side_send, side_recv, 1)
    solver_factor(1)
    solver_solve(1)
    particular(1, second_rhs)
    left, right = wait_back(1)
    for k in range(N):
        value = part[1, k] + from_left[1, k] * left + from_right[1, k] * right
        t_out[across(k), :] = value[0]
        h_out[across(k), :] = value[1]

    for n in range(2):
        z_copy[n].wait_send()
    pl.when(gy < N - 1)(y_up.wait_send)
    pl.when(gy > 0)(y_down.wait_send)
    for d in range(2):
        sent_to_solvers(d, coef_send, 0)
        sent_to_solvers(d, side_send, 1)
        pl.when(axes[d]["solves"])(
            lambda d=d: wait_slots(back_send.at[d], axes[d]["served"] - 1, net_sem.at[d, 2, 0])
        )


def body(*args):
    flat = [a.reshape(N * N, LANES) for a in args]
    block = (N * N, LANES)
    rows = (N, 2, N, LANES)
    both = (2, N, 2, N, LANES)
    vmem = lambda *shape: pltpu.VMEM(shape, F32)
    outs = pl.pallas_call(
        kernel,
        out_shape=[jax.ShapeDtypeStruct(block, F32)] * 2,
        in_specs=[pl.BlockSpec(memory_space=pltpu.HBM)] * 8,
        out_specs=[pl.BlockSpec(memory_space=pltpu.VMEM)] * 2,
        scratch_shapes=[
            vmem(2, *block),
            *[vmem(*block)] * 6,
            vmem(2, *block), vmem(*rows), vmem(2, *block),
            *[vmem(*both)] * 8,
            vmem(*rows), vmem(*rows),
            vmem(2, 2, N, LANES), vmem(2, 2, N, LANES),
            vmem(2, N, LANES), vmem(2, N, LANES),
            vmem(2, SOLVERS, 4, 8, LANES), vmem(2, N, 4, 8, LANES),
            vmem(2, SOLVERS, 2, 8, LANES), vmem(2, N, 2, 8, LANES),
            vmem(2, N, 2, 8, LANES), vmem(2, SOLVERS, 2, 8, LANES),
            vmem(2, N, 6, 8, LANES),
            pltpu.SemaphoreType.DMA((8,)),
            pltpu.SemaphoreType.DMA((2, 2)), pltpu.SemaphoreType.DMA((2, 2)),
            pltpu.SemaphoreType.DMA((2, 3, 2)), pltpu.SemaphoreType.REGULAR((3,)),
        ],
        compiler_params=pltpu.CompilerParams(
            collective_id=0, has_side_effects=True, vmem_limit_bytes=56229888
        ),
    )(*flat)
    return tuple(o.reshape(N, N, LANES) for o in outs)


def solution(mesh):
    spec = P("gx", "gy", "gz")
    return jax.shard_map(
        body, mesh=mesh, in_specs=(spec,) * 8, out_specs=(spec,) * 2, check_vma=False
    )
```

```python
import functools

import jax
import jax.numpy as jnp
from jax import lax
from jax.experimental import pallas as pl
from jax.experimental.pallas import tpu as pltpu
from jax.sharding import PartitionSpec as P

vapour_scaling = 0.8
N = 16
LANES = 128
SOLVERS = 4
MESH = pl.DeviceIdType.MESH
F32 = jnp.float32


def kernel(
    t_in, h_in, load_in, k_in, kz_in, cx_in, cy_in, cz_in,
    t_out, h_out,
    fields, load, mix, mix_z, cfl_x, cfl_y, cfl_z,
    side, mask_z, half,
    first_w, last_w, inv, wi, ratio_c, from_left, from_right, part,
    tmp_a, tmp_b,
    y_send, y_face, z_send, z_face, pull_send, pull, extra_send, extra,
    coef_send, coef_recv, side_send, side_recv, back_send, back_recv, lu,
    in_sem, y_sem, z_sem, net_sem, pull_sem, extra_sem, far_sem,
):
    gx, gy, gz = lax.axis_index("gx"), lax.axis_index("gy"), lax.axis_index("gz")
    core = lax.rem(gx, 2)

    tile_x = lax.rem(lax.div(gx, 2), 4)
    tile_y = lax.rem(lax.div(gy, 2), 4)
    axes = (
        dict(
            me=gx, tile=tile_x, solves=gx == 8 * lax.rem(tile_x, 2) + 2 * tile_x,
            solvers=lambda s: (8 * (s % 2) + 2 * s,), device=lambda i: (i, gy, gz),
            served=N, serve=lambda i: i,
        ),
        dict(
            me=gy, tile=tile_y, solves=lax.rem(gy, 2) == core,
            solvers=lambda s: (2 * s + core, N // 2 + 2 * s + core), device=lambda i: (gx, i, gz),
            served=N // 2, serve=lambda i: lax.rem(gy + N - N // 4 + i, N),
        ),
    )

    loads = [
        pltpu.make_async_copy(src, dst, in_sem.at[n])
        for n, (src, dst) in enumerate((
            (k_in, mix), (cx_in, cfl_x), (t_in, fields.at[0]), (h_in, fields.at[1]),
            (cy_in, cfl_y), (kz_in, mix_z), (cz_in, cfl_z), (load_in, load),
        ))
    ]
    for copy in loads:
        copy.start()

    def ring(step):
        return (gx, lax.rem(gy + step + N, N), gz)

    def signal(sem, device):
        pl.semaphore_signal(sem, inc=1, device_id=device, device_id_type=MESH)

    barrier = pltpu.get_barrier_semaphore()
    signal(barrier, (gx, gy, 1 - gz))
    signal(barrier, ring(1))
    signal(barrier, ring(-1))
    for s in range(SOLVERS):
        (solver,) = axes[0]["solvers"](s)
        pl.when(gx != solver)(functools.partial(signal, barrier, axes[0]["device"](solver)))

    @pl.when(axes[0]["solves"])
    def _():
        @pl.loop(0, N)
        def _(i):
            pl.when(i != gx)(lambda: signal(barrier, axes[0]["device"](i)))

    expected = 3 + jnp.where(axes[0]["solves"], N - 1 + SOLVERS - 1, SOLVERS)

    def tell(r):
        signal(far_sem.at[r], ring(1 << r))
        signal(far_sem.at[r], ring(-(1 << r)))

    def hear(r):
        pl.semaphore_wait(far_sem.at[r], 2)

    lane = lax.broadcasted_iota(jnp.int32, (2, N, LANES), 2)
    field = lax.broadcasted_iota(jnp.int32, (2, N, LANES), 0)
    ratio = jnp.where(field == 0, 1.0, vapour_scaling).astype(F32)
    weight = jnp.where(field == 0, 1.0, 0.0).astype(F32)
    lane2 = lax.broadcasted_iota(jnp.int32, (N, LANES), 1)
    face = jnp.where(gz == 0, LANES - 1, 0)

    def along(n):
        return pl.ds(N * n, N)

    def across(n):
        return pl.ds(n, N, stride=N)

    def pair(ref, rows):
        return jnp.broadcast_to(ref[rows, :][None], (2, N, LANES))

    def pack_column(rows, y, packed):
        for f in range(2):
            n = 1 + N * f + y
            moved = pltpu.roll(rows[f], n + 1 - gz, 1)
            packed = jnp.where(lane2 == n, moved, packed)
        return packed

    def unpack_column(packed, y):
        return jnp.stack(
            [pltpu.roll(packed, LANES - 1 - (1 + N * f + y) + gz, 1) for f in range(2)]
        )

    def factor(d, rows, cfl):
        def bands(k):
            mixed = ratio * pair(mix, rows(k))
            speed = 0.5 * pair(cfl, rows(k))
            return mixed - speed, mixed + speed

        rest, chain = None, None
        for k in range(N):
            east, west = bands(k)
            v = 1.0 + (west if rest is None else west * rest)
            i = 1.0 / (v + east)
            c = east * i
            rest = v * i
            w = west * i
            chain = w if chain is None else w * chain
            inv[d, k] = i
            wi[d, k] = w
            ratio_c[d, k] = c
            tmp_a[k] = chain
        q, t, prod = chain, c, None
        from_left[d, N - 1] = q
        from_right[d, N - 1] = t
        ends = [None, None, q, t]
        for k in range(N - 1, -1, -1):
            if k < N - 1:
                c = ratio_c[d, k]
                q = tmp_a[k] + c * q
                t = c * t
                from_left[d, k] = q
                from_right[d, k] = t
        ends[0], ends[1] = q, t
        for v, value in enumerate(ends):
            for s in range(SOLVERS):
                coef_send[d, s, v] = value[s // 2, 8 * (s % 2) : 8 * (s % 2) + 8]

    def weights(d, rows, cfl):
        def bands(k):
            mixed = ratio * pair(mix, rows(k))
            speed = 0.5 * pair(cfl, rows(k))
            return mixed - speed, mixed + speed

        rest, prod = None, None
        for k in range(N - 1, -1, -1):
            east, west = bands(k)
            v = 1.0 + (east if rest is None else east * rest)
            i = 1.0 / (v + west)
            rest = v * i
            tmp_a[k] = i
            tmp_b[k] = east * i
            last_w[d, k] = inv[d, k] if prod is None else inv[d, k] * prod
            prod = wi[d, k] if prod is None else wi[d, k] * prod
        prod = None
        for k in range(N):
            first_w[d, k] = tmp_a[k] if prod is None else tmp_a[k] * prod
            prod = tmp_b[k] if prod is None else tmp_b[k] * prod

    def to_solvers(d, send, recv, kind):
        ax = axes[d]
        for s in range(SOLVERS):
            for solver in ax["solvers"](s):
                copy = pltpu.make_async_remote_copy(
                    send.at[d, s], recv.at[d, ax["me"]],
                    net_sem.at[d, kind, 0], net_sem.at[d, kind, 1],
                    device_id=ax["device"](solver), device_id_type=MESH,
                )
                pl.when(ax["me"] != solver)(copy.start)

                @pl.when(ax["me"] == solver)
                def _():
                    recv[d, ax["me"]] = send[d, s]

    def wait_slots(ref, count, sem):
        pltpu.make_async_copy(ref.at[pl.ds(0, count)], ref.at[pl.ds(0, count)], sem).wait()

    def sent_to_solvers(d, send, kind):
        for _ in axes[d]["solvers"](0)[1:]:
            wait_slots(send.at[d], SOLVERS, net_sem.at[d, kind, 0])
        pl.when(axes[d]["solves"])(
            lambda: wait_slots(send.at[d], SOLVERS - 1, net_sem.at[d, kind, 0])
        )
        pl.when(jnp.logical_not(axes[d]["solves"]))(
            lambda: wait_slots(send.at[d], SOLVERS, net_sem.at[d, kind, 0])
        )

    def solver_factor(d):
        @pl.when(axes[d]["solves"])
        def _():
            wait_slots(coef_recv.at[d], N - 1, net_sem.at[d, 0, 1])
            beta = None
            for i in range(N):
                q0, t0, q1, t1 = (coef_recv[d, i, v] for v in range(4))
                if beta is None:
                    dinv = jnp.ones_like(q0)
                    b = jnp.zeros_like(q0)
                    tau = t0
                    beta = t1
                    a = b
                    dq = b
                else:
                    dinv = 1.0 / (1.0 - q0 * beta)
                    b = q1 * beta * dinv
                    tau = t0 * dinv
                    beta = t1 + b * t0
                    a = q1 + b * q0
                    dq = dinv * q0
                for n, value in enumerate((dinv, dq, a, b, tau, beta)):
                    lu[d, i, n] = value

    def solver_solve(d):
        ax = axes[d]

        @pl.when(ax["solves"])
        def _():
            wait_slots(side_recv.at[d], N - 1, net_sem.at[d, 1, 1])
            if d == 1:
                wait_slots(extra, N, extra_sem.at[1])
            on_face = lane2[:8] == face
            start = 2 * N * lax.div(ax["tile"], 2) + 8 * lax.rem(ax["tile"], 2)
            spot = lane2[:8] - start - lax.broadcasted_iota(jnp.int32, (8, LANES), 0)
            alpha, alphas, phis = None, [], []
            for i in range(N):
                p0, p1 = side_recv[d, i, 0], side_recv[d, i, 1]
                if d == 1:
                    sent = jnp.broadcast_to(extra[i], (8, LANES))
                    d0, d1 = (
                        jnp.sum(jnp.where(spot == N * v, sent, 0.0), axis=1, keepdims=True) for v in range(2)
                    )
                    p0 = p0 + jnp.where(on_face, d0, 0.0)
                    p1 = p1 + jnp.where(on_face, d1, 0.0)
                if alpha is None:
                    phi, alpha = p0, p1
                else:
                    phi = lu[d, i, 0] * p0 + lu[d, i, 1] * alpha
                    alpha = (p1 + lu[d, i, 3] * p0) + lu[d, i, 2] * alpha
                alphas.append(alpha)
                phis.append(phi)
            zero = jnp.zeros((8, LANES), F32)
            first, firsts, lasts = zero, [None] * N, [None] * N
            for i in range(N - 1, -1, -1):
                lasts[i] = alphas[i] + lu[d, i, 5] * first
                first = phis[i] + lu[d, i, 4] * first
                firsts[i] = first
            for i in range(N):
                back_send[d, i, 0] = lasts[i - 1] if i > 0 else zero
                back_send[d, i, 1] = firsts[i + 1] if i < N - 1 else zero

            @pl.loop(0, ax["served"])
            def _(i):
                j = ax["serve"](i)
                copy = pltpu.make_async_remote_copy(
                    back_send.at[d, j], back_recv.at[d, ax["tile"]],
                    net_sem.at[d, 2, 0], net_sem.at[d, 2, 1],
                    device_id=ax["device"](j), device_id_type=MESH,
                )
                pl.when(j != ax["me"])(copy.start)

            back_recv[d, ax["tile"]] = back_send[d, ax["me"]]

    def wait_back(d):
        pl.when(axes[d]["solves"])(
            lambda: wait_slots(back_recv.at[d], SOLVERS - 1, net_sem.at[d, 2, 1])
        )
        pl.when(jnp.logical_not(axes[d]["solves"]))(
            lambda: wait_slots(back_recv.at[d], SOLVERS, net_sem.at[d, 2, 1])
        )
        return tuple(
            back_recv[d, :, v].reshape(2, N, LANES) for v in range(2)
        )

    def ends_of(d, rhs):
        sums = [None, None]
        for k in range(N):
            b = rhs(k)
            terms = first_w[d, k] * b, last_w[d, k] * b
            sums = [x if s is None else s + x for s, x in zip(sums, terms)]
        for v in range(2):
            for s in range(SOLVERS):
                side_send[d, s, v] = sums[v][s // 2, 8 * (s % 2) : 8 * (s % 2) + 8]

    def particular(d, rhs):
        g = None
        for k in range(N):
            g = inv[d, k] * rhs(k) + (0.0 if g is None else wi[d, k] * g)
            tmp_a[k] = g
        value = g
        part[d, N - 1] = value
        for k in range(N - 2, -1, -1):
            value = tmp_a[k] + ratio_c[d, k] * value
            part[d, k] = value

    loads[0].wait()
    loads[1].wait()
    factor(0, along, cfl_x)

    loads[2].wait()
    loads[3].wait()
    y_send[0] = fields[:, across(0), :]
    y_send[1] = fields[:, across(N - 1), :]
    packed = jnp.zeros((N, LANES), F32)
    for y in range(N):
        packed = pack_column(fields[:, across(y), :], y, packed)
    z_send[0] = packed
    pl.when(gy == 0)(lambda: y_face.__setitem__(0, jnp.zeros((2, N, LANES), F32)))
    pl.when(gy == N - 1)(lambda: y_face.__setitem__(1, jnp.zeros((2, N, LANES), F32)))

    pl.semaphore_wait(barrier, expected)

    z_copy = [
        pltpu.make_async_remote_copy(
            z_send.at[n], z_face.at[n], z_sem.at[n, 0], z_sem.at[n, 1],
            device_id=(gx, gy, 1 - gz), device_id_type=MESH,
        )
        for n in range(2)
    ]
    y_up = pltpu.make_async_remote_copy(
        y_send.at[1], y_face.at[0], y_sem.at[0, 0], y_sem.at[0, 1],
        device_id=(gx, gy + 1, gz), device_id_type=MESH,
    )
    y_down = pltpu.make_async_remote_copy(
        y_send.at[0], y_face.at[1], y_sem.at[1, 0], y_sem.at[1, 1],
        device_id=(gx, gy - 1, gz), device_id_type=MESH,
    )
    z_copy[0].start()
    pl.when(gy < N - 1)(y_up.start)
    pl.when(gy > 0)(y_down.start)
    to_solvers(0, coef_send, coef_recv, 0)
    tell(0)

    weights(0, along, cfl_x)

    for n in range(4, 8):
        loads[n].wait()
    toward = jnp.where(gz == 0, -0.5, 0.5).astype(F32)

    def vertical(v, y):
        mixed = ratio * pair(mix_z, across(y))
        cfl = pair(cfl_z, across(y))
        up = jnp.where(lane == LANES - 1, 0.0, pltpu.roll(v, LANES - 1, 2))
        down = jnp.where(lane == 0, 0.0, pltpu.roll(v, 1, 2))
        return (mixed - 0.5 * cfl) * (up - v) + (mixed + 0.5 * cfl) * (down - v)

    edge_coef = [None, None]
    for y in range(N):
        here = fields[:, across(y), :]
        mixed = ratio * pair(mix, across(y))
        speed = 0.5 * pair(cfl_y, across(y))
        east, west = mixed - speed, mixed + speed
        ahead = fields[:, across(y + 1), :] - here if y < N - 1 else -here
        behind = fields[:, across(y - 1), :] - here if y > 0 else -here
        value = here + (east * ahead + west * behind) + vertical(here, y)
        value = value + weight * pair(load, across(y))
        side[:, along(y), :] = value
        outward = ratio * pair(mix_z, across(y)) + toward * pair(cfl_z, across(y))
        mask_z[y] = jnp.where(lane == face, outward, 0.0)
        if y == 0:
            edge_coef[0] = west
        if y == N - 1:
            edge_coef[1] = east

    factor(1, across, cfl_y)
    weights(1, across, cfl_y)

    for v, ws in enumerate((first_w, last_w)):
        packed = jnp.zeros((N, LANES), F32)
        for y in range(N):
            packed = pack_column(ws[1, y] * mask_z[y], y, packed)
        pull_send[v] = packed
    pull_copy = pltpu.make_async_remote_copy(
        pull_send, pull, pull_sem.at[0], pull_sem.at[1],
        device_id=(gx, gy, 1 - gz), device_id_type=MESH,
    )
    pull_copy.start()
    hear(0)
    tell(1)

    z_copy[0].wait_recv()
    pl.when(gy > 0)(y_up.wait_recv)
    pl.when(gy < N - 1)(y_down.wait_recv)
    got = z_face[0]
    for y in range(N):
        value = side[:, along(y), :] + mask_z[y] * unpack_column(got, y)
        if y == 0:
            value = value + edge_coef[0] * y_face[0]
        if y == N - 1:
            value = value + edge_coef[1] * y_face[1]
        side[:, along(y), :] = value

    def first_rhs(k):
        return side[:, across(k), :]

    ends_of(0, first_rhs)
    to_solvers(0, side_send, side_recv, 1)
    hear(1)
    tell(2)
    solver_factor(0)
    solver_solve(0)
    particular(0, first_rhs)
    hear(2)
    signal(far_sem.at[3], (gx, gy, 1 - gz))
    to_solvers(1, coef_send, coef_recv, 0)
    left, right = wait_back(0)
    for k in range(N):
        half[:, along(k), :] = part[0, k] + from_left[0, k] * left + from_right[0, k] * right

    packed = jnp.zeros((N, LANES), F32)
    for y in range(N):
        packed = pack_column(half[:, across(y), :], y, packed)
    z_send[1] = packed
    z_copy[1].start()

    pull_copy.wait_recv()
    sums = [pull[v] * packed for v in range(2)]
    row = lax.broadcasted_iota(jnp.int32, (N, LANES), 0)
    spread = jnp.zeros((N, LANES), F32)
    for f in range(2):
        mine = jnp.logical_and(lane2 > N * f, lane2 <= N * f + N)
        for v in range(2):
            total = jnp.sum(jnp.where(mine, sums[v], 0.0), axis=1, keepdims=True)
            spread = jnp.where(lane2 == N * (2 * f + v) + row, total, spread)
    extra_send[0] = jnp.sum(spread, axis=0, keepdims=True)
    pl.semaphore_wait(far_sem.at[3], 1)
    for s in range(SOLVERS):
        for solver in axes[1]["solvers"](s):
            pltpu.make_async_remote_copy(
                extra_send.at[0], extra.at[gy], extra_sem.at[0], extra_sem.at[1],
                device_id=(gx, solver, 1 - gz), device_id_type=MESH,
            ).start()

    for y in range(N):
        here = half[:, across(y), :]
        value = 2.0 * here - side[:, along(y), :] + vertical(here, y)
        side[:, along(y), :] = value + weight * pair(load, across(y))

    def second_rhs(k):
        return side[:, along(k), :]

    ends_of(1, second_rhs)
    to_solvers(1, side_send, side_recv, 1)
    z_copy[1].wait_recv()
    got = z_face[1]
    for y in range(N):
        side[:, along(y), :] = side[:, along(y), :] + mask_z[y] * unpack_column(got, y)
    particular(1, second_rhs)
    solver_factor(1)
    solver_solve(1)
    left, right = wait_back(1)
    for k in range(N):
        value = part[1, k] + from_left[1, k] * left + from_right[1, k] * right
        t_out[across(k), :] = value[0]
        h_out[across(k), :] = value[1]

    for n in range(2):
        z_copy[n].wait_send()
    for _ in range(2 * SOLVERS):
        wait_slots(extra_send, 1, extra_sem.at[0])
    pull_copy.wait_send()
    pl.when(gy < N - 1)(y_up.wait_send)
    pl.when(gy > 0)(y_down.wait_send)
    for d in range(2):
        sent_to_solvers(d, coef_send, 0)
        sent_to_solvers(d, side_send, 1)
        pl.when(axes[d]["solves"])(
            lambda d=d: wait_slots(back_send.at[d], axes[d]["served"] - 1, net_sem.at[d, 2, 0])
        )


def body(*args):
    flat = [a.reshape(N * N, LANES) for a in args]
    block = (N * N, LANES)
    rows = (N, 2, N, LANES)
    both = (2, N, 2, N, LANES)
    vmem = lambda *shape: pltpu.VMEM(shape, F32)
    outs = pl.pallas_call(
        kernel,
        out_shape=[jax.ShapeDtypeStruct(block, F32)] * 2,
        in_specs=[pl.BlockSpec(memory_space=pltpu.HBM)] * 8,
        out_specs=[pl.BlockSpec(memory_space=pltpu.VMEM)] * 2,
        scratch_shapes=[
            vmem(2, *block),
            *[vmem(*block)] * 6,
            vmem(2, *block), vmem(*rows), vmem(2, *block),
            *[vmem(*both)] * 8,
            vmem(*rows), vmem(*rows),
            vmem(2, 2, N, LANES), vmem(2, 2, N, LANES),
            vmem(2, N, LANES), vmem(2, N, LANES),
            vmem(2, N, LANES), vmem(2, N, LANES),
            vmem(1, 1, LANES), vmem(N, 1, LANES),
            vmem(2, SOLVERS, 4, 8, LANES), vmem(2, N, 4, 8, LANES),
            vmem(2, SOLVERS, 2, 8, LANES), vmem(2, N, 2, 8, LANES),
            vmem(2, N, 2, 8, LANES), vmem(2, SOLVERS, 2, 8, LANES),
            vmem(2, N, 6, 8, LANES),
            pltpu.SemaphoreType.DMA((8,)),
            pltpu.SemaphoreType.DMA((2, 2)), pltpu.SemaphoreType.DMA((2, 2)),
            pltpu.SemaphoreType.DMA((2, 3, 2)), pltpu.SemaphoreType.DMA((2,)),
            pltpu.SemaphoreType.DMA((2,)), pltpu.SemaphoreType.REGULAR((4,)),
        ],
        compiler_params=pltpu.CompilerParams(
            collective_id=0, has_side_effects=True, vmem_limit_bytes=56229888
        ),
    )(*flat)
    return tuple(o.reshape(N, N, LANES) for o in outs)


def solution(mesh):
    spec = P("gx", "gy", "gz")
    return jax.shard_map(
        body, mesh=mesh, in_specs=(spec,) * 8, out_specs=(spec,) * 2, check_vma=False
    )
```

```python
import functools

import jax
import jax.numpy as jnp
from jax import lax
from jax.experimental import pallas as pl
from jax.experimental.pallas import tpu as pltpu
from jax.sharding import PartitionSpec as P

vapour_scaling = 0.8
N = 16
LANES = 128
SOLVERS = 4
MESH = pl.DeviceIdType.MESH
F32 = jnp.float32


def kernel(
    t_in, h_in, load_in, k_in, kz_in, cx_in, cy_in, cz_in,
    t_out, h_out,
    fields, load, mix, mix_z, cfl_x, cfl_y, cfl_z,
    side, mask_z, half,
    first_w, last_w, inv, wi, ratio_c, from_left, from_right, part,
    tmp_a, tmp_b,
    y_send, y_face, z_send, z_face, pull_send, pull, extra_send, extra,
    coef_send, coef_recv, side_send, side_recv, back_send, back_recv, lu,
    in_sem, y_sem, z_sem, net_sem, pull_sem, extra_sem, far_sem,
):
    gx, gy, gz = lax.axis_index("gx"), lax.axis_index("gy"), lax.axis_index("gz")
    core = lax.rem(gx, 2)

    half_x, chip_x = lax.div(gx, N // 2), lax.rem(lax.div(gx, 2), 4)
    odd = lax.rem(gy + core, 2)

    def solver_x(other_half, step):
        chip = lax.rem(chip_x + step, 4)
        return chip, N // 2 * lax.rem(half_x + other_half, 2) + 2 * chip

    def solver_y(step):
        j = lax.rem(gy + step - odd + N, N)
        return lax.rem(lax.div(j, 2), 4), j

    axes = (
        dict(
            me=gx, tile=chip_x, solves=core == 0, device=lambda i: (i, gy, gz),
            solvers=[solver_x(*step) for step in ((1, 2), (1, 1), (1, 3), (0, 2), (1, 0), (0, 1), (0, 3), (0, 0))],
            served=[
                N // 2 * half_x + 2 * lax.rem(chip_x + step, 4) + c
                for step, c in ((2, 1), (2, 0), (1, 1), (3, 1), (1, 0), (3, 0), (0, 1))
            ],
        ),
        dict(
            me=gy, tile=lax.rem(lax.div(gy, 2), 4), solves=odd == 0, device=lambda i: (gx, i, gz),
            solvers=[solver_y(step) for step in (8, -6, 6, -4, 4, -2, 2, 0)],
            served=[lax.rem(gy + step + N, N) for step in (-4, 3, -3, 2, -2, 1, -1)],
        ),
    )

    loads = [
        pltpu.make_async_copy(src, dst, in_sem.at[n])
        for n, (src, dst) in enumerate((
            (k_in, mix), (cx_in, cfl_x), (t_in, fields.at[0]), (h_in, fields.at[1]),
            (cy_in, cfl_y), (kz_in, mix_z), (cz_in, cfl_z), (load_in, load),
        ))
    ]
    for copy in loads:
        copy.start()

    def ring(step):
        return (gx, lax.rem(gy + step + N, N), gz)

    def signal(sem, device):
        pl.semaphore_signal(sem, inc=1, device_id=device, device_id_type=MESH)

    barrier = pltpu.get_barrier_semaphore()
    signal(barrier, (gx, gy, 1 - gz))
    for step in (1, -1, 2, -2):
        signal(barrier, ring(step))
    for _, solver in axes[0]["solvers"]:
        pl.when(gx != solver)(functools.partial(signal, barrier, axes[0]["device"](solver)))

    @pl.when(axes[0]["solves"])
    def _():
        @pl.loop(0, N)
        def _(i):
            pl.when(i != gx)(lambda: signal(barrier, axes[0]["device"](i)))

    expected = 5 + jnp.where(axes[0]["solves"], N - 1 + 2 * SOLVERS - 1, 2 * SOLVERS)

    def tell(r):
        signal(far_sem.at[r], ring(2 << r))
        signal(far_sem.at[r], ring(-(2 << r)))

    def hear(r):
        pl.semaphore_wait(far_sem.at[r], 2)

    lane = lax.broadcasted_iota(jnp.int32, (2, N, LANES), 2)
    field = lax.broadcasted_iota(jnp.int32, (2, N, LANES), 0)
    ratio = jnp.where(field == 0, 1.0, vapour_scaling).astype(F32)
    weight = jnp.where(field == 0, 1.0, 0.0).astype(F32)
    lane2 = lax.broadcasted_iota(jnp.int32, (N, LANES), 1)
    face = jnp.where(gz == 0, LANES - 1, 0)

    def along(n):
        return pl.ds(N * n, N)

    def across(n):
        return pl.ds(n, N, stride=N)

    def pair(ref, rows):
        return jnp.broadcast_to(ref[rows, :][None], (2, N, LANES))

    def pack_column(rows, y, packed):
        for f in range(2):
            n = 1 + N * f + y
            moved = pltpu.roll(rows[f], n + 1 - gz, 1)
            packed = jnp.where(lane2 == n, moved, packed)
        return packed

    def unpack_column(packed, y):
        return jnp.stack(
            [pltpu.roll(packed, LANES - 1 - (1 + N * f + y) + gz, 1) for f in range(2)]
        )

    def factor(d, rows, cfl):
        def bands(k):
            mixed = ratio * pair(mix, rows(k))
            speed = 0.5 * pair(cfl, rows(k))
            return mixed - speed, mixed + speed

        rest, chain = None, None
        for k in range(N):
            east, west = bands(k)
            v = 1.0 + (west if rest is None else west * rest)
            i = 1.0 / (v + east)
            c = east * i
            rest = v * i
            w = west * i
            chain = w if chain is None else w * chain
            inv[d, k] = i
            wi[d, k] = w
            ratio_c[d, k] = c
            tmp_a[k] = chain
        q, t, prod = chain, c, None
        from_left[d, N - 1] = q
        from_right[d, N - 1] = t
        ends = [None, None, q, t]
        for k in range(N - 1, -1, -1):
            if k < N - 1:
                c = ratio_c[d, k]
                q = tmp_a[k] + c * q
                t = c * t
                from_left[d, k] = q
                from_right[d, k] = t
        ends[0], ends[1] = q, t
        for v, value in enumerate(ends):
            for s in range(SOLVERS):
                coef_send[d, s, v] = value[s // 2, 8 * (s % 2) : 8 * (s % 2) + 8]

    def weights(d, rows, cfl):
        def bands(k):
            mixed = ratio * pair(mix, rows(k))
            speed = 0.5 * pair(cfl, rows(k))
            return mixed - speed, mixed + speed

        rest, prod = None, None
        for k in range(N - 1, -1, -1):
            east, west = bands(k)
            v = 1.0 + (east if rest is None else east * rest)
            i = 1.0 / (v + west)
            rest = v * i
            tmp_a[k] = i
            tmp_b[k] = east * i
            last_w[d, k] = inv[d, k] if prod is None else inv[d, k] * prod
            prod = wi[d, k] if prod is None else wi[d, k] * prod
        prod = None
        for k in range(N):
            first_w[d, k] = tmp_a[k] if prod is None else tmp_a[k] * prod
            prod = tmp_b[k] if prod is None else tmp_b[k] * prod

    def to_solvers(d, send, recv, kind):
        ax = axes[d]
        for s, solver in ax["solvers"]:
            copy = pltpu.make_async_remote_copy(
                send.at[d, s], recv.at[d, ax["me"]],
                net_sem.at[d, kind, 0], net_sem.at[d, kind, 1],
                device_id=ax["device"](solver), device_id_type=MESH,
            )
            pl.when(ax["me"] != solver)(copy.start)

        @pl.when(ax["solves"])
        def _():
            recv[d, ax["me"]] = send[d, ax["tile"]]

    def wait_slots(ref, count, sem):
        pltpu.make_async_copy(ref.at[pl.ds(0, count)], ref.at[pl.ds(0, count)], sem).wait()

    def sent_to_solvers(d, send, kind):
        wait_slots(send.at[d], SOLVERS, net_sem.at[d, kind, 0])
        pl.when(axes[d]["solves"])(
            lambda: wait_slots(send.at[d], SOLVERS - 1, net_sem.at[d, kind, 0])
        )
        pl.when(jnp.logical_not(axes[d]["solves"]))(
            lambda: wait_slots(send.at[d], SOLVERS, net_sem.at[d, kind, 0])
        )

    def solver_factor(d):
        @pl.when(axes[d]["solves"])
        def _():
            wait_slots(coef_recv.at[d], N - 1, net_sem.at[d, 0, 1])
            beta = None
            for i in range(N):
                q0, t0, q1, t1 = (coef_recv[d, i, v] for v in range(4))
                if beta is None:
                    dinv = jnp.ones_like(q0)
                    b = jnp.zeros_like(q0)
                    tau = t0
                    beta = t1
                    a = b
                    dq = b
                else:
                    dinv = 1.0 / (1.0 - q0 * beta)
                    b = q1 * beta * dinv
                    tau = t0 * dinv
                    beta = t1 + b * t0
                    a = q1 + b * q0
                    dq = dinv * q0
                for n, value in enumerate((dinv, dq, a, b, tau, beta)):
                    lu[d, i, n] = value

    def solver_solve(d):
        ax = axes[d]

        @pl.when(ax["solves"])
        def _():
            wait_slots(side_recv.at[d], N - 1, net_sem.at[d, 1, 1])
            if d == 1:
                wait_slots(extra, N, extra_sem.at[1])
            on_face = lane2[:8] == face
            start = 2 * N * lax.div(ax["tile"], 2) + 8 * lax.rem(ax["tile"], 2)
            spot = lane2[:8] - start - lax.broadcasted_iota(jnp.int32, (8, LANES), 0)
            alpha, alphas, phis = None, [], []
            for i in range(N):
                p0, p1 = side_recv[d, i, 0], side_recv[d, i, 1]
                if d == 1:
                    sent = jnp.broadcast_to(extra[i], (8, LANES))
                    d0, d1 = (
                        jnp.sum(jnp.where(spot == N * v, sent, 0.0), axis=1, keepdims=True) for v in range(2)
                    )
                    p0 = p0 + jnp.where(on_face, d0, 0.0)
                    p1 = p1 + jnp.where(on_face, d1, 0.0)
                if alpha is None:
                    phi, alpha = p0, p1
                else:
                    phi = lu[d, i, 0] * p0 + lu[d, i, 1] * alpha
                    alpha = (p1 + lu[d, i, 3] * p0) + lu[d, i, 2] * alpha
                alphas.append(alpha)
                phis.append(phi)
            zero = jnp.zeros((8, LANES), F32)
            first, firsts, lasts = zero, [None] * N, [None] * N
            for i in range(N - 1, -1, -1):
                lasts[i] = alphas[i] + lu[d, i, 5] * first
                first = phis[i] + lu[d, i, 4] * first
                firsts[i] = first
            for i in range(N):
                back_send[d, i, 0] = lasts[i - 1] if i > 0 else zero
                back_send[d, i, 1] = firsts[i + 1] if i < N - 1 else zero

            for j in ax["served"]:
                pltpu.make_async_remote_copy(
                    back_send.at[d, j], back_recv.at[d, ax["tile"]],
                    net_sem.at[d, 2, 0], net_sem.at[d, 2, 1],
                    device_id=ax["device"](j), device_id_type=MESH,
                ).start()

            back_recv[d, ax["tile"]] = back_send[d, ax["me"]]

    def wait_back(d):
        pl.when(axes[d]["solves"])(
            lambda: wait_slots(back_recv.at[d], SOLVERS - 1, net_sem.at[d, 2, 1])
        )
        pl.when(jnp.logical_not(axes[d]["solves"]))(
            lambda: wait_slots(back_recv.at[d], SOLVERS, net_sem.at[d, 2, 1])
        )
        return tuple(
            back_recv[d, :, v].reshape(2, N, LANES) for v in range(2)
        )

    def ends_of(d, rhs):
        sums = [None, None]
        for k in range(N):
            b = rhs(k)
            terms = first_w[d, k] * b, last_w[d, k] * b
            sums = [x if s is None else s + x for s, x in zip(sums, terms)]
        for v in range(2):
            for s in range(SOLVERS):
                side_send[d, s, v] = sums[v][s // 2, 8 * (s % 2) : 8 * (s % 2) + 8]

    def particular(d, rhs):
        g = None
        for k in range(N):
            g = inv[d, k] * rhs(k) + (0.0 if g is None else wi[d, k] * g)
            tmp_a[k] = g
        value = g
        part[d, N - 1] = value
        for k in range(N - 2, -1, -1):
            value = tmp_a[k] + ratio_c[d, k] * value
            part[d, k] = value

    loads[0].wait()
    loads[1].wait()
    factor(0, along, cfl_x)

    loads[2].wait()
    loads[3].wait()
    y_send[0] = fields[:, across(0), :]
    y_send[1] = fields[:, across(N - 1), :]
    packed = jnp.zeros((N, LANES), F32)
    for y in range(N):
        packed = pack_column(fields[:, across(y), :], y, packed)
    z_send[0] = packed
    pl.when(gy == 0)(lambda: y_face.__setitem__(0, jnp.zeros((2, N, LANES), F32)))
    pl.when(gy == N - 1)(lambda: y_face.__setitem__(1, jnp.zeros((2, N, LANES), F32)))

    pl.semaphore_wait(barrier, expected)

    z_copy = [
        pltpu.make_async_remote_copy(
            z_send.at[n], z_face.at[n], z_sem.at[n, 0], z_sem.at[n, 1],
            device_id=(gx, gy, 1 - gz), device_id_type=MESH,
        )
        for n in range(2)
    ]
    y_up = pltpu.make_async_remote_copy(
        y_send.at[1], y_face.at[0], y_sem.at[0, 0], y_sem.at[0, 1],
        device_id=(gx, gy + 1, gz), device_id_type=MESH,
    )
    y_down = pltpu.make_async_remote_copy(
        y_send.at[0], y_face.at[1], y_sem.at[1, 0], y_sem.at[1, 1],
        device_id=(gx, gy - 1, gz), device_id_type=MESH,
    )
    z_copy[0].start()
    pl.when(gy < N - 1)(y_up.start)
    pl.when(gy > 0)(y_down.start)
    to_solvers(0, coef_send, coef_recv, 0)
    tell(0)

    weights(0, along, cfl_x)

    for n in range(4, 8):
        loads[n].wait()
    toward = jnp.where(gz == 0, -0.5, 0.5).astype(F32)

    def vertical(v, y):
        mixed = ratio * pair(mix_z, across(y))
        cfl = pair(cfl_z, across(y))
        up = jnp.where(lane == LANES - 1, 0.0, pltpu.roll(v, LANES - 1, 2))
        down = jnp.where(lane == 0, 0.0, pltpu.roll(v, 1, 2))
        return (mixed - 0.5 * cfl) * (up - v) + (mixed + 0.5 * cfl) * (down - v)

    edge_coef = [None, None]
    for y in range(N):
        here = fields[:, across(y), :]
        mixed = ratio * pair(mix, across(y))
        speed = 0.5 * pair(cfl_y, across(y))
        east, west = mixed - speed, mixed + speed
        ahead = fields[:, across(y + 1), :] - here if y < N - 1 else -here
        behind = fields[:, across(y - 1), :] - here if y > 0 else -here
        value = here + (east * ahead + west * behind) + vertical(here, y)
        value = value + weight * pair(load, across(y))
        side[:, along(y), :] = value
        outward = ratio * pair(mix_z, across(y)) + toward * pair(cfl_z, across(y))
        mask_z[y] = jnp.where(lane == face, outward, 0.0)
        if y == 0:
            edge_coef[0] = west
        if y == N - 1:
            edge_coef[1] = east

    factor(1, across, cfl_y)
    weights(1, across, cfl_y)

    for v, ws in enumerate((first_w, last_w)):
        packed = jnp.zeros((N, LANES), F32)
        for y in range(N):
            packed = pack_column(ws[1, y] * mask_z[y], y, packed)
        pull_send[v] = packed
    pull_copy = pltpu.make_async_remote_copy(
        pull_send, pull, pull_sem.at[0], pull_sem.at[1],
        device_id=(gx, gy, 1 - gz), device_id_type=MESH,
    )
    pull_copy.start()
    hear(0)
    tell(1)

    z_copy[0].wait_recv()
    pl.when(gy > 0)(y_up.wait_recv)
    pl.when(gy < N - 1)(y_down.wait_recv)
    got = z_face[0]
    for y in range(N):
        value = side[:, along(y), :] + mask_z[y] * unpack_column(got, y)
        if y == 0:
            value = value + edge_coef[0] * y_face[0]
        if y == N - 1:
            value = value + edge_coef[1] * y_face[1]
        side[:, along(y), :] = value

    def first_rhs(k):
        return side[:, across(k), :]

    ends_of(0, first_rhs)
    to_solvers(0, side_send, side_recv, 1)
    solver_factor(0)
    hear(1)
    signal(far_sem.at[2], (gx, gy, 1 - gz))
    to_solvers(1, coef_send, coef_recv, 0)
    solver_solve(0)
    particular(0, first_rhs)
    left, right = wait_back(0)
    for k in range(N):
        half[:, along(k), :] = part[0, k] + from_left[0, k] * left + from_right[0, k] * right

    packed = jnp.zeros((N, LANES), F32)
    for y in range(N):
        packed = pack_column(half[:, across(y), :], y, packed)
    z_send[1] = packed
    z_copy[1].start()

    pull_copy.wait_recv()
    sums = [pull[v] * packed for v in range(2)]
    row = lax.broadcasted_iota(jnp.int32, (N, LANES), 0)
    spread = jnp.zeros((N, LANES), F32)
    for f in range(2):
        mine = jnp.logical_and(lane2 > N * f, lane2 <= N * f + N)
        for v in range(2):
            total = jnp.sum(jnp.where(mine, sums[v], 0.0), axis=1, keepdims=True)
            spread = jnp.where(lane2 == N * (2 * f + v) + row, total, spread)
    extra_send[0] = jnp.sum(spread, axis=0, keepdims=True)
    pl.semaphore_wait(far_sem.at[2], 1)
    for _, solver in axes[1]["solvers"]:
        pltpu.make_async_remote_copy(
            extra_send.at[0], extra.at[gy], extra_sem.at[0], extra_sem.at[1],
            device_id=(gx, solver, 1 - gz), device_id_type=MESH,
        ).start()

    for y in range(N):
        here = half[:, across(y), :]
        value = 2.0 * here - side[:, along(y), :] + vertical(here, y)
        side[:, along(y), :] = value + weight * pair(load, across(y))

    def second_rhs(k):
        return side[:, along(k), :]

    ends_of(1, second_rhs)
    to_solvers(1, side_send, side_recv, 1)
    z_copy[1].wait_recv()
    got = z_face[1]
    for y in range(N):
        side[:, along(y), :] = side[:, along(y), :] + mask_z[y] * unpack_column(got, y)
    particular(1, second_rhs)
    solver_factor(1)
    solver_solve(1)
    left, right = wait_back(1)
    for k in range(N):
        value = part[1, k] + from_left[1, k] * left + from_right[1, k] * right
        t_out[across(k), :] = value[0]
        h_out[across(k), :] = value[1]

    for n in range(2):
        z_copy[n].wait_send()
    for _ in range(2 * SOLVERS):
        wait_slots(extra_send, 1, extra_sem.at[0])
    pull_copy.wait_send()
    pl.when(gy < N - 1)(y_up.wait_send)
    pl.when(gy > 0)(y_down.wait_send)
    for d in range(2):
        sent_to_solvers(d, coef_send, 0)
        sent_to_solvers(d, side_send, 1)
        pl.when(axes[d]["solves"])(
            lambda d=d: wait_slots(back_send.at[d], len(axes[d]["served"]), net_sem.at[d, 2, 0])
        )


def body(*args):
    flat = [a.reshape(N * N, LANES) for a in args]
    block = (N * N, LANES)
    rows = (N, 2, N, LANES)
    both = (2, N, 2, N, LANES)
    vmem = lambda *shape: pltpu.VMEM(shape, F32)
    outs = pl.pallas_call(
        kernel,
        out_shape=[jax.ShapeDtypeStruct(block, F32)] * 2,
        in_specs=[pl.BlockSpec(memory_space=pltpu.HBM)] * 8,
        out_specs=[pl.BlockSpec(memory_space=pltpu.VMEM)] * 2,
        scratch_shapes=[
            vmem(2, *block),
            *[vmem(*block)] * 6,
            vmem(2, *block), vmem(*rows), vmem(2, *block),
            *[vmem(*both)] * 8,
            vmem(*rows), vmem(*rows),
            vmem(2, 2, N, LANES), vmem(2, 2, N, LANES),
            vmem(2, N, LANES), vmem(2, N, LANES),
            vmem(2, N, LANES), vmem(2, N, LANES),
            vmem(1, 1, LANES), vmem(N, 1, LANES),
            vmem(2, SOLVERS, 4, 8, LANES), vmem(2, N, 4, 8, LANES),
            vmem(2, SOLVERS, 2, 8, LANES), vmem(2, N, 2, 8, LANES),
            vmem(2, N, 2, 8, LANES), vmem(2, SOLVERS, 2, 8, LANES),
            vmem(2, N, 6, 8, LANES),
            pltpu.SemaphoreType.DMA((8,)),
            pltpu.SemaphoreType.DMA((2, 2)), pltpu.SemaphoreType.DMA((2, 2)),
            pltpu.SemaphoreType.DMA((2, 3, 2)), pltpu.SemaphoreType.DMA((2,)),
            pltpu.SemaphoreType.DMA((2,)), pltpu.SemaphoreType.REGULAR((3,)),
        ],
        compiler_params=pltpu.CompilerParams(
            collective_id=0, has_side_effects=True, vmem_limit_bytes=56229888
        ),
    )(*flat)
    return tuple(o.reshape(N, N, LANES) for o in outs)


def solution(mesh):
    spec = P("gx", "gy", "gz")
    return jax.shard_map(
        body, mesh=mesh, in_specs=(spec,) * 8, out_specs=(spec,) * 2, check_vma=False
    )
```

```python
import functools

import jax
import jax.numpy as jnp
from jax import lax
from jax.experimental import pallas as pl
from jax.experimental.pallas import tpu as pltpu
from jax.sharding import PartitionSpec as P

vapour_scaling = 0.8
N = 16
LANES = 128
SOLVERS = 4
MESH = pl.DeviceIdType.MESH
F32 = jnp.float32


def kernel(
    t_in, h_in, load_in, k_in, kz_in, cx_in, cy_in, cz_in,
    t_out, h_out, one_out,
    fields, load, mix, mix_z, cfl_x, cfl_y, cfl_z,
    side, mask_z, half,
    first_w, last_w, inv, wi, ratio_c, from_left, from_right, part,
    tmp_a, tmp_b,
    y_send, y_face, z_send, z_face, pull_send, pull, extra_send, extra,
    coef_send, coef_recv, side_send, side_recv, back_send, back_recv, lu,
    in_sem, y_sem, z_sem, net_sem, pull_sem, extra_sem, far_sem,
):
    gx, gy, gz = lax.axis_index("gx"), lax.axis_index("gy"), lax.axis_index("gz")
    core = lax.rem(gx, 2)

    half_x, chip_x = lax.div(gx, N // 2), lax.rem(lax.div(gx, 2), 4)
    odd = lax.rem(gy + core, 2)

    def solver_x(other_half, step):
        chip = lax.rem(chip_x + step, 4)
        return chip, N // 2 * lax.rem(half_x + other_half, 2) + 2 * chip

    def solver_y(step):
        j = lax.rem(gy + step - odd + N, N)
        return lax.rem(lax.div(j, 2), 4), j

    axes = (
        dict(
            me=gx, tile=chip_x, solves=core == 0, device=lambda i: (i, gy, gz),
            solvers=[solver_x(*step) for step in ((1, 2), (1, 1), (1, 3), (0, 2), (1, 0), (0, 1), (0, 3), (0, 0))],
            served=[
                N // 2 * half_x + 2 * lax.rem(chip_x + step, 4) + c
                for step, c in ((2, 1), (2, 0), (1, 1), (3, 1), (1, 0), (3, 0), (0, 1))
            ],
        ),
        dict(
            me=gy, tile=lax.rem(lax.div(gy, 2), 4), solves=odd == 0, device=lambda i: (gx, i, gz),
            solvers=[solver_y(step) for step in (8, -6, 6, -4, 4, -2, 2, 0)],
            served=[lax.rem(gy + step + N, N) for step in (4, -3, 3, -2, 2, -1, 1)],
        ),
    )

    loads = [
        pltpu.make_async_copy(src, dst, in_sem.at[n])
        for n, (src, dst) in enumerate((
            (k_in, mix), (cx_in, cfl_x), (t_in, fields.at[0]), (h_in, fields.at[1]),
            (cy_in, cfl_y), (kz_in, mix_z), (cz_in, cfl_z), (load_in, load),
        ))
    ]
    for copy in loads:
        copy.start()

    def ring(step):
        return (gx, lax.rem(gy + step + N, N), gz)

    def signal(sem, device):
        pl.semaphore_signal(sem, inc=1, device_id=device, device_id_type=MESH)

    barrier = pltpu.get_barrier_semaphore()
    signal(barrier, (gx, gy, 1 - gz))
    for step in (1, -1, 2, -2):
        signal(barrier, ring(step))
    for _, solver in axes[0]["solvers"]:
        pl.when(gx != solver)(functools.partial(signal, barrier, axes[0]["device"](solver)))

    @pl.when(axes[0]["solves"])
    def _():
        @pl.loop(0, N)
        def _(i):
            pl.when(i != gx)(lambda: signal(barrier, axes[0]["device"](i)))

    expected = 5 + jnp.where(axes[0]["solves"], N - 1 + 2 * SOLVERS - 1, 2 * SOLVERS)

    def tell(r):
        signal(far_sem.at[r], ring(2 << r))
        signal(far_sem.at[r], ring(-(2 << r)))

    def hear(r):
        pl.semaphore_wait(far_sem.at[r], 2)

    lane = lax.broadcasted_iota(jnp.int32, (2, N, LANES), 2)
    field = lax.broadcasted_iota(jnp.int32, (2, N, LANES), 0)
    ratio = jnp.where(field == 0, 1.0, vapour_scaling).astype(F32)
    weight = jnp.where(field == 0, 1.0, 0.0).astype(F32)
    lane2 = lax.broadcasted_iota(jnp.int32, (N, LANES), 1)
    face = jnp.where(gz == 0, LANES - 1, 0)

    def along(n):
        return pl.ds(N * n, N)

    def across(n):
        return pl.ds(n, N, stride=N)

    def pair(ref, rows):
        return jnp.broadcast_to(ref[rows, :][None], (2, N, LANES))

    def pack_column(rows, y, packed):
        for f in range(2):
            n = 1 + N * f + y
            moved = pltpu.roll(rows[f], n + 1 - gz, 1)
            packed = jnp.where(lane2 == n, moved, packed)
        return packed

    def unpack_column(packed, y):
        return jnp.stack(
            [pltpu.roll(packed, LANES - 1 - (1 + N * f + y) + gz, 1) for f in range(2)]
        )

    def factor(d, rows, cfl):
        def bands(k):
            mixed = ratio * pair(mix, rows(k))
            speed = 0.5 * pair(cfl, rows(k))
            return mixed - speed, mixed + speed

        rest, chain = None, None
        for k in range(N):
            east, west = bands(k)
            v = 1.0 + (west if rest is None else west * rest)
            i = 1.0 / (v + east)
            c = east * i
            rest = v * i
            w = west * i
            chain = w if chain is None else w * chain
            inv[d, k] = i
            wi[d, k] = w
            ratio_c[d, k] = c
            tmp_a[k] = chain
        q, t, prod = chain, c, None
        from_left[d, N - 1] = q
        from_right[d, N - 1] = t
        ends = [None, None, q, t]
        for k in range(N - 1, -1, -1):
            if k < N - 1:
                c = ratio_c[d, k]
                q = tmp_a[k] + c * q
                t = c * t
                from_left[d, k] = q
                from_right[d, k] = t
        ends[0], ends[1] = q, t
        for v, value in enumerate(ends):
            for s in range(SOLVERS):
                coef_send[d, s, v] = value[s // 2, 8 * (s % 2) : 8 * (s % 2) + 8]

    def weights(d, rows, cfl):
        def bands(k):
            mixed = ratio * pair(mix, rows(k))
            speed = 0.5 * pair(cfl, rows(k))
            return mixed - speed, mixed + speed

        rest, prod = None, None
        for k in range(N - 1, -1, -1):
            east, west = bands(k)
            v = 1.0 + (east if rest is None else east * rest)
            i = 1.0 / (v + west)
            rest = v * i
            tmp_a[k] = i
            tmp_b[k] = east * i
            last_w[d, k] = inv[d, k] if prod is None else inv[d, k] * prod
            prod = wi[d, k] if prod is None else wi[d, k] * prod
        prod = None
        for k in range(N):
            first_w[d, k] = tmp_a[k] if prod is None else tmp_a[k] * prod
            prod = tmp_b[k] if prod is None else tmp_b[k] * prod

    def to_solvers(d, send, recv, kind):
        ax = axes[d]
        for s, solver in ax["solvers"]:
            copy = pltpu.make_async_remote_copy(
                send.at[d, s], recv.at[d, ax["me"]],
                net_sem.at[d, kind, 0], net_sem.at[d, kind, 1],
                device_id=ax["device"](solver), device_id_type=MESH,
            )
            pl.when(ax["me"] != solver)(copy.start)

        @pl.when(ax["solves"])
        def _():
            recv[d, ax["me"]] = send[d, ax["tile"]]

    def wait_slots(ref, count, sem):
        pltpu.make_async_copy(ref.at[pl.ds(0, count)], ref.at[pl.ds(0, count)], sem).wait()

    def sent_to_solvers(d, send, kind):
        wait_slots(send.at[d], SOLVERS, net_sem.at[d, kind, 0])
        pl.when(axes[d]["solves"])(
            lambda: wait_slots(send.at[d], SOLVERS - 1, net_sem.at[d, kind, 0])
        )
        pl.when(jnp.logical_not(axes[d]["solves"]))(
            lambda: wait_slots(send.at[d], SOLVERS, net_sem.at[d, kind, 0])
        )

    def solver_factor(d):
        @pl.when(axes[d]["solves"])
        def _():
            wait_slots(coef_recv.at[d], N - 1, net_sem.at[d, 0, 1])
            beta = None
            for i in range(N):
                q0, t0, q1, t1 = (coef_recv[d, i, v] for v in range(4))
                if beta is None:
                    dinv = jnp.ones_like(q0)
                    b = jnp.zeros_like(q0)
                    tau = t0
                    beta = t1
                    a = b
                    dq = b
                else:
                    dinv = 1.0 / (1.0 - q0 * beta)
                    b = q1 * beta * dinv
                    tau = t0 * dinv
                    beta = t1 + b * t0
                    a = q1 + b * q0
                    dq = dinv * q0
                for n, value in enumerate((dinv, dq, a, b, tau, beta)):
                    lu[d, i, n] = value

    def solver_solve(d):
        ax = axes[d]

        @pl.when(ax["solves"])
        def _():
            wait_slots(side_recv.at[d], N - 1, net_sem.at[d, 1, 1])
            if d == 1:
                wait_slots(extra, N, extra_sem.at[1])
            on_face = lane2[:8] == face
            start = 2 * N * lax.div(ax["tile"], 2) + 8 * lax.rem(ax["tile"], 2)
            spot = lane2[:8] - start - lax.broadcasted_iota(jnp.int32, (8, LANES), 0)
            alpha, alphas, phis = None, [], []
            for i in range(N):
                p0, p1 = side_recv[d, i, 0], side_recv[d, i, 1]
                if d == 1:
                    sent = jnp.broadcast_to(extra[i], (8, LANES))
                    d0, d1 = (
                        jnp.sum(jnp.where(spot == N * v, sent, 0.0), axis=1, keepdims=True) for v in range(2)
                    )
                    p0 = p0 + jnp.where(on_face, d0, 0.0)
                    p1 = p1 + jnp.where(on_face, d1, 0.0)
                if alpha is None:
                    phi, alpha = p0, p1
                else:
                    phi = lu[d, i, 0] * p0 + lu[d, i, 1] * alpha
                    alpha = (p1 + lu[d, i, 3] * p0) + lu[d, i, 2] * alpha
                alphas.append(alpha)
                phis.append(phi)
            zero = jnp.zeros((8, LANES), F32)
            first, firsts, lasts = zero, [None] * N, [None] * N
            for i in range(N - 1, -1, -1):
                lasts[i] = alphas[i] + lu[d, i, 5] * first
                first = phis[i] + lu[d, i, 4] * first
                firsts[i] = first
            for i in range(N):
                back_send[d, i, 0] = lasts[i - 1] if i > 0 else zero
                back_send[d, i, 1] = firsts[i + 1] if i < N - 1 else zero

            for j in ax["served"]:
                pltpu.make_async_remote_copy(
                    back_send.at[d, j], back_recv.at[d, ax["tile"]],
                    net_sem.at[d, 2, 0], net_sem.at[d, 2, 1],
                    device_id=ax["device"](j), device_id_type=MESH,
                ).start()

            back_recv[d, ax["tile"]] = back_send[d, ax["me"]]

    def wait_back(d):
        pl.when(axes[d]["solves"])(
            lambda: wait_slots(back_recv.at[d], SOLVERS - 1, net_sem.at[d, 2, 1])
        )
        pl.when(jnp.logical_not(axes[d]["solves"]))(
            lambda: wait_slots(back_recv.at[d], SOLVERS, net_sem.at[d, 2, 1])
        )
        return tuple(
            back_recv[d, :, v].reshape(2, N, LANES) for v in range(2)
        )

    def ends_of(d, rhs):
        sums = [None, None]
        for k in range(N):
            b = rhs(k)
            terms = first_w[d, k] * b, last_w[d, k] * b
            sums = [x if s is None else s + x for s, x in zip(sums, terms)]
        for v in range(2):
            for s in range(SOLVERS):
                side_send[d, s, v] = sums[v][s // 2, 8 * (s % 2) : 8 * (s % 2) + 8]

    def particular(d, rhs):
        g = None
        for k in range(N):
            g = inv[d, k] * rhs(k) + (0.0 if g is None else wi[d, k] * g)
            tmp_a[k] = g
        value = g
        part[d, N - 1] = value
        for k in range(N - 2, -1, -1):
            value = tmp_a[k] + ratio_c[d, k] * value
            part[d, k] = value

    loads[0].wait()
    loads[1].wait()
    factor(0, along, cfl_x)

    loads[2].wait()
    loads[3].wait()
    y_send[0] = fields[:, across(0), :]
    y_send[1] = fields[:, across(N - 1), :]
    packed = jnp.zeros((N, LANES), F32)
    for y in range(N):
        packed = pack_column(fields[:, across(y), :], y, packed)
    z_send[0] = packed
    pl.when(gy == 0)(lambda: y_face.__setitem__(0, jnp.zeros((2, N, LANES), F32)))
    pl.when(gy == N - 1)(lambda: y_face.__setitem__(1, jnp.zeros((2, N, LANES), F32)))

    pl.semaphore_wait(barrier, expected)

    z_copy = [
        pltpu.make_async_remote_copy(
            z_send.at[n], z_face.at[n], z_sem.at[n, 0], z_sem.at[n, 1],
            device_id=(gx, gy, 1 - gz), device_id_type=MESH,
        )
        for n in range(2)
    ]
    y_up = pltpu.make_async_remote_copy(
        y_send.at[1], y_face.at[0], y_sem.at[0, 0], y_sem.at[0, 1],
        device_id=(gx, gy + 1, gz), device_id_type=MESH,
    )
    y_down = pltpu.make_async_remote_copy(
        y_send.at[0], y_face.at[1], y_sem.at[1, 0], y_sem.at[1, 1],
        device_id=(gx, gy - 1, gz), device_id_type=MESH,
    )
    z_copy[0].start()
    pl.when(gy < N - 1)(y_up.start)
    pl.when(gy > 0)(y_down.start)
    to_solvers(0, coef_send, coef_recv, 0)
    tell(0)

    weights(0, along, cfl_x)

    for n in range(4, 8):
        loads[n].wait()
    toward = jnp.where(gz == 0, -0.5, 0.5).astype(F32)

    def vertical(v, y):
        mixed = ratio * pair(mix_z, across(y))
        cfl = pair(cfl_z, across(y))
        up = jnp.where(lane == LANES - 1, 0.0, pltpu.roll(v, LANES - 1, 2))
        down = jnp.where(lane == 0, 0.0, pltpu.roll(v, 1, 2))
        return (mixed - 0.5 * cfl) * (up - v) + (mixed + 0.5 * cfl) * (down - v)

    edge_coef = [None, None]
    for y in range(N):
        here = fields[:, across(y), :]
        mixed = ratio * pair(mix, across(y))
        speed = 0.5 * pair(cfl_y, across(y))
        east, west = mixed - speed, mixed + speed
        ahead = fields[:, across(y + 1), :] - here if y < N - 1 else -here
        behind = fields[:, across(y - 1), :] - here if y > 0 else -here
        value = here + (east * ahead + west * behind) + vertical(here, y)
        value = value + weight * pair(load, across(y))
        side[:, along(y), :] = value
        outward = ratio * pair(mix_z, across(y)) + toward * pair(cfl_z, across(y))
        mask_z[y] = jnp.where(lane == face, outward, 0.0)
        if y == 0:
            edge_coef[0] = west
        if y == N - 1:
            edge_coef[1] = east

    factor(1, across, cfl_y)
    weights(1, across, cfl_y)

    for v, ws in enumerate((first_w, last_w)):
        packed = jnp.zeros((N, LANES), F32)
        for y in range(N):
            packed = pack_column(ws[1, y] * mask_z[y], y, packed)
        pull_send[v] = packed
    pull_copy = pltpu.make_async_remote_copy(
        pull_send, pull, pull_sem.at[0], pull_sem.at[1],
        device_id=(gx, gy, 1 - gz), device_id_type=MESH,
    )
    pull_copy.start()
    hear(0)
    tell(1)

    z_copy[0].wait_recv()
    pl.when(gy > 0)(y_up.wait_recv)
    pl.when(gy < N - 1)(y_down.wait_recv)
    got = z_face[0]
    for y in range(N):
        value = side[:, along(y), :] + mask_z[y] * unpack_column(got, y)
        if y == 0:
            value = value + edge_coef[0] * y_face[0]
        if y == N - 1:
            value = value + edge_coef[1] * y_face[1]
        side[:, along(y), :] = value

    def first_rhs(k):
        return side[:, across(k), :]

    ends_of(0, first_rhs)
    to_solvers(0, side_send, side_recv, 1)
    solver_factor(0)
    hear(1)
    signal(far_sem.at[2], (gx, gy, 1 - gz))
    to_solvers(1, coef_send, coef_recv, 0)
    solver_solve(0)
    particular(0, first_rhs)
    left, right = wait_back(0)
    for k in range(N):
        half[:, along(k), :] = part[0, k] + from_left[0, k] * left + from_right[0, k] * right

    packed = jnp.zeros((N, LANES), F32)
    for y in range(N):
        packed = pack_column(half[:, across(y), :], y, packed)
    z_send[1] = packed
    z_copy[1].start()

    pull_copy.wait_recv()
    sums = [pull[v] * packed for v in range(2)]
    row = lax.broadcasted_iota(jnp.int32, (N, LANES), 0)
    spread = jnp.zeros((N, LANES), F32)
    for f in range(2):
        mine = jnp.logical_and(lane2 > N * f, lane2 <= N * f + N)
        for v in range(2):
            total = jnp.sum(jnp.where(mine, sums[v], 0.0), axis=1, keepdims=True)
            spread = jnp.where(lane2 == N * (2 * f + v) + row, total, spread)
    extra_send[0] = jnp.sum(spread, axis=0, keepdims=True)
    pl.semaphore_wait(far_sem.at[2], 1)
    for _, solver in axes[1]["solvers"]:
        pltpu.make_async_remote_copy(
            extra_send.at[0], extra.at[gy], extra_sem.at[0], extra_sem.at[1],
            device_id=(gx, solver, 1 - gz), device_id_type=MESH,
        ).start()

    for y in range(N):
        here = half[:, across(y), :]
        value = 2.0 * here - side[:, along(y), :] + vertical(here, y)
        side[:, along(y), :] = value + weight * pair(load, across(y))

    def second_rhs(k):
        return side[:, along(k), :]

    ends_of(1, second_rhs)
    to_solvers(1, side_send, side_recv, 1)
    z_copy[1].wait_recv()
    got = z_face[1]
    for y in range(N):
        side[:, along(y), :] = side[:, along(y), :] + mask_z[y] * unpack_column(got, y)
    particular(1, second_rhs)
    solver_factor(1)
    solver_solve(1)
    left, right = wait_back(1)
    one_out[...] = jnp.ones((N, LANES), F32)
    for k in range(N):
        value = part[1, k] + from_left[1, k] * left + from_right[1, k] * right
        t_out[across(k), :] = value[0]
        h_out[across(k), :] = value[1]

    for n in range(2):
        z_copy[n].wait_send()
    for _ in range(2 * SOLVERS):
        wait_slots(extra_send, 1, extra_sem.at[0])
    pull_copy.wait_send()
    pl.when(gy < N - 1)(y_up.wait_send)
    pl.when(gy > 0)(y_down.wait_send)
    for d in range(2):
        sent_to_solvers(d, coef_send, 0)
        sent_to_solvers(d, side_send, 1)
        pl.when(axes[d]["solves"])(
            lambda d=d: wait_slots(back_send.at[d], len(axes[d]["served"]), net_sem.at[d, 2, 0])
        )


def body(*args):
    flat = [a.reshape(N * N, LANES) for a in args]
    block = (N * N, LANES)
    rows = (N, 2, N, LANES)
    both = (2, N, 2, N, LANES)
    vmem = lambda *shape: pltpu.VMEM(shape, F32)
    outs = pl.pallas_call(
        kernel,
        out_shape=[jax.ShapeDtypeStruct(block, F32)] * 2 + [jax.ShapeDtypeStruct((N, LANES), F32)],
        in_specs=[pl.BlockSpec(memory_space=pltpu.HBM)] * 8,
        out_specs=[pl.BlockSpec(memory_space=pltpu.VMEM)] * 3,
        scratch_shapes=[
            vmem(2, *block),
            *[vmem(*block)] * 6,
            vmem(2, *block), vmem(*rows), vmem(2, *block),
            *[vmem(*both)] * 8,
            vmem(*rows), vmem(*rows),
            vmem(2, 2, N, LANES), vmem(2, 2, N, LANES),
            vmem(2, N, LANES), vmem(2, N, LANES),
            vmem(2, N, LANES), vmem(2, N, LANES),
            vmem(1, 1, LANES), vmem(N, 1, LANES),
            vmem(2, SOLVERS, 4, 8, LANES), vmem(2, N, 4, 8, LANES),
            vmem(2, SOLVERS, 2, 8, LANES), vmem(2, N, 2, 8, LANES),
            vmem(2, N, 2, 8, LANES), vmem(2, SOLVERS, 2, 8, LANES),
            vmem(2, N, 6, 8, LANES),
            pltpu.SemaphoreType.DMA((8,)),
            pltpu.SemaphoreType.DMA((2, 2)), pltpu.SemaphoreType.DMA((2, 2)),
            pltpu.SemaphoreType.DMA((2, 3, 2)), pltpu.SemaphoreType.DMA((2,)),
            pltpu.SemaphoreType.DMA((2,)), pltpu.SemaphoreType.REGULAR((3,)),
        ],
        compiler_params=pltpu.CompilerParams(
            collective_id=0, has_side_effects=True, vmem_limit_bytes=56229888
        ),
    )(*flat)
    return tuple(o.reshape(N, N, LANES) * outs[2][None] for o in outs[:2])


def solution(mesh):
    spec = P("gx", "gy", "gz")
    return jax.shard_map(
        body, mesh=mesh, in_specs=(spec,) * 8, out_specs=(spec,) * 2, check_vma=False
    )
```

```python
import functools

import jax
import jax.numpy as jnp
from jax import lax
from jax.experimental import pallas as pl
from jax.experimental.pallas import tpu as pltpu
from jax.sharding import PartitionSpec as P

vapour_scaling = 0.8
N = 16
LANES = 128
SOLVERS = 4
MESH = pl.DeviceIdType.MESH
F32 = jnp.float32


def kernel(
    t_in, h_in, load_in, k_in, kz_in, cx_in, cy_in, cz_in,
    t_out, h_out, one_out,
    fields, load, mix, mix_z, cfl_x, cfl_y, cfl_z,
    side, mask_z, half,
    first_w, last_w, inv, wi, ratio_c, from_left, from_right, part,
    tmp_a, tmp_b,
    y_send, y_face, z_send, z_face, pull_send, pull, extra_send, extra,
    coef_send, coef_recv, side_send, side_recv, back_send, back_recv, lu,
    in_sem, y_sem, z_sem, net_sem, pull_sem, extra_sem, far_sem,
):
    gx, gy, gz = lax.axis_index("gx"), lax.axis_index("gy"), lax.axis_index("gz")
    core = lax.rem(gx, 2)

    half_x, chip_x = lax.div(gx, N // 2), lax.rem(lax.div(gx, 2), 4)
    odd = lax.rem(gy + core, 2)

    def solver_x(other_half, step):
        chip = lax.rem(chip_x + step, 4)
        return chip, N // 2 * lax.rem(half_x + other_half, 2) + 2 * chip

    def solver_y(step):
        j = lax.rem(gy + step - odd + N, N)
        return lax.rem(lax.div(j, 2), 4), j

    axes = (
        dict(
            me=gx, tile=chip_x, solves=core == 0, device=lambda i: (i, gy, gz),
            solvers=[solver_x(*step) for step in ((1, 2), (1, 1), (1, 3), (0, 2), (1, 0), (0, 1), (0, 3), (0, 0))],
            served=[
                N // 2 * half_x + 2 * lax.rem(chip_x + step, 4) + c
                for step, c in ((2, 1), (2, 0), (1, 1), (3, 1), (1, 0), (3, 0), (0, 1))
            ],
        ),
        dict(
            me=gy, tile=lax.rem(lax.div(gy, 2), 4), solves=odd == 0, device=lambda i: (gx, i, gz),
            solvers=[solver_y(step) for step in (8, -6, 6, -4, 4, -2, 2, 0)],
            served=[lax.rem(gy + step + N, N) for step in (4, -3, 3, -2, 2, -1, 1)],
        ),
    )

    loads = [
        pltpu.make_async_copy(src, dst, in_sem.at[n])
        for n, (src, dst) in enumerate((
            (k_in, mix), (cx_in, cfl_x), (t_in, fields.at[0]), (h_in, fields.at[1]),
            (cy_in, cfl_y), (kz_in, mix_z), (cz_in, cfl_z), (load_in, load),
        ))
    ]
    for copy in loads:
        copy.start()

    def ring(step):
        return (gx, lax.rem(gy + step + N, N), gz)

    def signal(sem, device):
        pl.semaphore_signal(sem, inc=1, device_id=device, device_id_type=MESH)

    barrier = pltpu.get_barrier_semaphore()
    signal(barrier, (gx, gy, 1 - gz))
    for step in (1, -1, 2, -2):
        signal(barrier, ring(step))

    @pl.when(axes[0]["solves"])
    def _():
        @pl.loop(1, N)
        def _(step):
            signal(barrier, axes[0]["device"](lax.rem(gx + step, N)))

    @pl.when(jnp.logical_not(axes[0]["solves"]))
    def _():
        for _, solver in axes[0]["solvers"]:
            signal(barrier, axes[0]["device"](solver))

    expected = 5 + jnp.where(axes[0]["solves"], N - 1, 2 * SOLVERS)

    def tell(r):
        signal(far_sem.at[r], ring(2 << r))
        signal(far_sem.at[r], ring(-(2 << r)))

    def hear(r):
        pl.semaphore_wait(far_sem.at[r], 2)

    lane = lax.broadcasted_iota(jnp.int32, (2, N, LANES), 2)
    field = lax.broadcasted_iota(jnp.int32, (2, N, LANES), 0)
    ratio = jnp.where(field == 0, 1.0, vapour_scaling).astype(F32)
    weight = jnp.where(field == 0, 1.0, 0.0).astype(F32)
    lane2 = lax.broadcasted_iota(jnp.int32, (N, LANES), 1)
    face = jnp.where(gz == 0, LANES - 1, 0)

    def along(n):
        return pl.ds(N * n, N)

    def across(n):
        return pl.ds(n, N, stride=N)

    def pair(ref, rows):
        return jnp.broadcast_to(ref[rows, :][None], (2, N, LANES))

    def pack_column(rows, y, packed):
        for f in range(2):
            n = 1 + N * f + y
            moved = pltpu.roll(rows[f], n + 1 - gz, 1)
            packed = jnp.where(lane2 == n, moved, packed)
        return packed

    def unpack_column(packed, y):
        return jnp.stack(
            [pltpu.roll(packed, LANES - 1 - (1 + N * f + y) + gz, 1) for f in range(2)]
        )

    def factor(d, rows, cfl):
        def bands(k):
            mixed = ratio * pair(mix, rows(k))
            speed = 0.5 * pair(cfl, rows(k))
            return mixed - speed, mixed + speed

        rest, chain = None, None
        for k in range(N):
            east, west = bands(k)
            v = 1.0 + (west if rest is None else west * rest)
            i = 1.0 / (v + east)
            c = east * i
            rest = v * i
            w = west * i
            chain = w if chain is None else w * chain
            inv[d, k] = i
            wi[d, k] = w
            ratio_c[d, k] = c
            tmp_a[k] = chain
        q, t, prod = chain, c, None
        from_left[d, N - 1] = q
        from_right[d, N - 1] = t
        ends = [None, None, q, t]
        for k in range(N - 1, -1, -1):
            if k < N - 1:
                c = ratio_c[d, k]
                q = tmp_a[k] + c * q
                t = c * t
                from_left[d, k] = q
                from_right[d, k] = t
        ends[0], ends[1] = q, t
        for v, value in enumerate(ends):
            for s in range(SOLVERS):
                coef_send[d, s, v] = value[s // 2, 8 * (s % 2) : 8 * (s % 2) + 8]

    def weights(d, rows, cfl):
        def bands(k):
            mixed = ratio * pair(mix, rows(k))
            speed = 0.5 * pair(cfl, rows(k))
            return mixed - speed, mixed + speed

        rest, prod = None, None
        for k in range(N - 1, -1, -1):
            east, west = bands(k)
            v = 1.0 + (east if rest is None else east * rest)
            i = 1.0 / (v + west)
            rest = v * i
            tmp_a[k] = i
            tmp_b[k] = east * i
            last_w[d, k] = inv[d, k] if prod is None else inv[d, k] * prod
            prod = wi[d, k] if prod is None else wi[d, k] * prod
        prod = None
        for k in range(N):
            first_w[d, k] = tmp_a[k] if prod is None else tmp_a[k] * prod
            prod = tmp_b[k] if prod is None else tmp_b[k] * prod

    def to_solvers(d, send, recv, kind):
        ax = axes[d]
        for s, solver in ax["solvers"]:
            copy = pltpu.make_async_remote_copy(
                send.at[d, s], recv.at[d, ax["me"]],
                net_sem.at[d, kind, 0], net_sem.at[d, kind, 1],
                device_id=ax["device"](solver), device_id_type=MESH,
            )
            pl.when(ax["me"] != solver)(copy.start)

        @pl.when(ax["solves"])
        def _():
            recv[d, ax["me"]] = send[d, ax["tile"]]

    def wait_slots(ref, count, sem):
        pltpu.make_async_copy(ref.at[pl.ds(0, count)], ref.at[pl.ds(0, count)], sem).wait()

    def sent_to_solvers(d, send, kind):
        wait_slots(send.at[d], SOLVERS, net_sem.at[d, kind, 0])
        pl.when(axes[d]["solves"])(
            lambda: wait_slots(send.at[d], SOLVERS - 1, net_sem.at[d, kind, 0])
        )
        pl.when(jnp.logical_not(axes[d]["solves"]))(
            lambda: wait_slots(send.at[d], SOLVERS, net_sem.at[d, kind, 0])
        )

    def solver_factor(d):
        @pl.when(axes[d]["solves"])
        def _():
            wait_slots(coef_recv.at[d], N - 1, net_sem.at[d, 0, 1])
            beta = None
            for i in range(N):
                q0, t0, q1, t1 = (coef_recv[d, i, v] for v in range(4))
                if beta is None:
                    dinv = jnp.ones_like(q0)
                    b = jnp.zeros_like(q0)
                    tau = t0
                    beta = t1
                    a = b
                    dq = b
                else:
                    dinv = 1.0 / (1.0 - q0 * beta)
                    b = q1 * beta * dinv
                    tau = t0 * dinv
                    beta = t1 + b * t0
                    a = q1 + b * q0
                    dq = dinv * q0
                for n, value in enumerate((dinv, dq, a, b, tau, beta)):
                    lu[d, i, n] = value

    def solver_solve(d):
        ax = axes[d]

        @pl.when(ax["solves"])
        def _():
            wait_slots(side_recv.at[d], N - 1, net_sem.at[d, 1, 1])
            if d == 1:
                wait_slots(extra, N, extra_sem.at[1])
            on_face = lane2[:8] == face
            start = 2 * N * lax.div(ax["tile"], 2) + 8 * lax.rem(ax["tile"], 2)
            spot = lane2[:8] - start - lax.broadcasted_iota(jnp.int32, (8, LANES), 0)
            alpha, alphas, phis = None, [], []
            for i in range(N):
                p0, p1 = side_recv[d, i, 0], side_recv[d, i, 1]
                if d == 1:
                    sent = jnp.broadcast_to(extra[i], (8, LANES))
                    d0, d1 = (
                        jnp.sum(jnp.where(spot == N * v, sent, 0.0), axis=1, keepdims=True) for v in range(2)
                    )
                    p0 = p0 + jnp.where(on_face, d0, 0.0)
                    p1 = p1 + jnp.where(on_face, d1, 0.0)
                if alpha is None:
                    phi, alpha = p0, p1
                else:
                    phi = lu[d, i, 0] * p0 + lu[d, i, 1] * alpha
                    alpha = (p1 + lu[d, i, 3] * p0) + lu[d, i, 2] * alpha
                alphas.append(alpha)
                phis.append(phi)
            zero = jnp.zeros((8, LANES), F32)
            first, firsts, lasts = zero, [None] * N, [None] * N
            for i in range(N - 1, -1, -1):
                lasts[i] = alphas[i] + lu[d, i, 5] * first
                first = phis[i] + lu[d, i, 4] * first
                firsts[i] = first
            for i in range(N):
                back_send[d, i, 0] = lasts[i - 1] if i > 0 else zero
                back_send[d, i, 1] = firsts[i + 1] if i < N - 1 else zero

            for j in ax["served"]:
                pltpu.make_async_remote_copy(
                    back_send.at[d, j], back_recv.at[d, ax["tile"]],
                    net_sem.at[d, 2, 0], net_sem.at[d, 2, 1],
                    device_id=ax["device"](j), device_id_type=MESH,
                ).start()

            back_recv[d, ax["tile"]] = back_send[d, ax["me"]]

    def wait_back(d):
        pl.when(axes[d]["solves"])(
            lambda: wait_slots(back_recv.at[d], SOLVERS - 1, net_sem.at[d, 2, 1])
        )
        pl.when(jnp.logical_not(axes[d]["solves"]))(
            lambda: wait_slots(back_recv.at[d], SOLVERS, net_sem.at[d, 2, 1])
        )
        return tuple(
            back_recv[d, :, v].reshape(2, N, LANES) for v in range(2)
        )

    def ends_of(d, rhs):
        sums = [None, None]
        for k in range(N):
            b = rhs(k)
            terms = first_w[d, k] * b, last_w[d, k] * b
            sums = [x if s is None else s + x for s, x in zip(sums, terms)]
        for v in range(2):
            for s in range(SOLVERS):
                side_send[d, s, v] = sums[v][s // 2, 8 * (s % 2) : 8 * (s % 2) + 8]

    def particular(d, rhs):
        g = None
        for k in range(N):
            g = inv[d, k] * rhs(k) + (0.0 if g is None else wi[d, k] * g)
            tmp_a[k] = g
        value = g
        part[d, N - 1] = value
        for k in range(N - 2, -1, -1):
            value = tmp_a[k] + ratio_c[d, k] * value
            part[d, k] = value

    loads[0].wait()
    loads[1].wait()
    factor(0, along, cfl_x)

    loads[2].wait()
    loads[3].wait()
    y_send[0] = fields[:, across(0), :]
    y_send[1] = fields[:, across(N - 1), :]
    packed = jnp.zeros((N, LANES), F32)
    for y in range(N):
        packed = pack_column(fields[:, across(y), :], y, packed)
    z_send[0] = packed
    pl.when(gy == 0)(lambda: y_face.__setitem__(0, jnp.zeros((2, N, LANES), F32)))
    pl.when(gy == N - 1)(lambda: y_face.__setitem__(1, jnp.zeros((2, N, LANES), F32)))

    pl.semaphore_wait(barrier, expected)

    z_copy = [
        pltpu.make_async_remote_copy(
            z_send.at[n], z_face.at[n], z_sem.at[n, 0], z_sem.at[n, 1],
            device_id=(gx, gy, 1 - gz), device_id_type=MESH,
        )
        for n in range(2)
    ]
    y_up = pltpu.make_async_remote_copy(
        y_send.at[1], y_face.at[0], y_sem.at[0, 0], y_sem.at[0, 1],
        device_id=(gx, gy + 1, gz), device_id_type=MESH,
    )
    y_down = pltpu.make_async_remote_copy(
        y_send.at[0], y_face.at[1], y_sem.at[1, 0], y_sem.at[1, 1],
        device_id=(gx, gy - 1, gz), device_id_type=MESH,
    )
    z_copy[0].start()
    pl.when(gy < N - 1)(y_up.start)
    pl.when(gy > 0)(y_down.start)
    tell(0)

    weights(0, along, cfl_x)

    for n in range(4, 8):
        loads[n].wait()
    toward = jnp.where(gz == 0, -0.5, 0.5).astype(F32)

    def vertical(v, y):
        mixed = ratio * pair(mix_z, across(y))
        cfl = pair(cfl_z, across(y))
        up = jnp.where(lane == LANES - 1, 0.0, pltpu.roll(v, LANES - 1, 2))
        down = jnp.where(lane == 0, 0.0, pltpu.roll(v, 1, 2))
        return (mixed - 0.5 * cfl) * (up - v) + (mixed + 0.5 * cfl) * (down - v)

    edge_coef = [None, None]
    for y in range(N):
        here = fields[:, across(y), :]
        mixed = ratio * pair(mix, across(y))
        speed = 0.5 * pair(cfl_y, across(y))
        east, west = mixed - speed, mixed + speed
        ahead = fields[:, across(y + 1), :] - here if y < N - 1 else -here
        behind = fields[:, across(y - 1), :] - here if y > 0 else -here
        value = here + (east * ahead + west * behind) + vertical(here, y)
        value = value + weight * pair(load, across(y))
        side[:, along(y), :] = value
        outward = ratio * pair(mix_z, across(y)) + toward * pair(cfl_z, across(y))
        mask_z[y] = jnp.where(lane == face, outward, 0.0)
        if y == 0:
            edge_coef[0] = west
        if y == N - 1:
            edge_coef[1] = east

    to_solvers(0, coef_send, coef_recv, 0)

    factor(1, across, cfl_y)
    weights(1, across, cfl_y)

    for v, ws in enumerate((first_w, last_w)):
        packed = jnp.zeros((N, LANES), F32)
        for y in range(N):
            packed = pack_column(ws[1, y] * mask_z[y], y, packed)
        pull_send[v] = packed
    pull_copy = pltpu.make_async_remote_copy(
        pull_send, pull, pull_sem.at[0], pull_sem.at[1],
        device_id=(gx, gy, 1 - gz), device_id_type=MESH,
    )
    pull_copy.start()
    hear(0)
    tell(1)

    z_copy[0].wait_recv()
    pl.when(gy > 0)(y_up.wait_recv)
    pl.when(gy < N - 1)(y_down.wait_recv)
    got = z_face[0]
    for y in range(N):
        value = side[:, along(y), :] + mask_z[y] * unpack_column(got, y)
        if y == 0:
            value = value + edge_coef[0] * y_face[0]
        if y == N - 1:
            value = value + edge_coef[1] * y_face[1]
        side[:, along(y), :] = value

    def first_rhs(k):
        return side[:, across(k), :]

    ends_of(0, first_rhs)
    to_solvers(0, side_send, side_recv, 1)
    solver_factor(0)
    hear(1)
    signal(far_sem.at[2], (gx, gy, 1 - gz))
    to_solvers(1, coef_send, coef_recv, 0)
    solver_solve(0)
    particular(0, first_rhs)
    left, right = wait_back(0)
    for k in range(N):
        half[:, along(k), :] = part[0, k] + from_left[0, k] * left + from_right[0, k] * right

    packed = jnp.zeros((N, LANES), F32)
    for y in range(N):
        packed = pack_column(half[:, across(y), :], y, packed)
    z_send[1] = packed
    z_copy[1].start()

    pull_copy.wait_recv()
    sums = [pull[v] * packed for v in range(2)]
    row = lax.broadcasted_iota(jnp.int32, (N, LANES), 0)
    spread = jnp.zeros((N, LANES), F32)
    for f in range(2):
        mine = jnp.logical_and(lane2 > N * f, lane2 <= N * f + N)
        for v in range(2):
            total = jnp.sum(jnp.where(mine, sums[v], 0.0), axis=1, keepdims=True)
            spread = jnp.where(lane2 == N * (2 * f + v) + row, total, spread)
    extra_send[0] = jnp.sum(spread, axis=0, keepdims=True)
    pl.semaphore_wait(far_sem.at[2], 1)
    for _, solver in axes[1]["solvers"]:
        pltpu.make_async_remote_copy(
            extra_send.at[0], extra.at[gy], extra_sem.at[0], extra_sem.at[1],
            device_id=(gx, solver, 1 - gz), device_id_type=MESH,
        ).start()

    for y in range(N):
        here = half[:, across(y), :]
        value = 2.0 * here - side[:, along(y), :] + vertical(here, y)
        side[:, along(y), :] = value + weight * pair(load, across(y))

    def second_rhs(k):
        return side[:, along(k), :]

    ends_of(1, second_rhs)
    to_solvers(1, side_send, side_recv, 1)
    z_copy[1].wait_recv()
    got = z_face[1]
    for y in range(N):
        side[:, along(y), :] = side[:, along(y), :] + mask_z[y] * unpack_column(got, y)
    particular(1, second_rhs)
    solver_factor(1)
    solver_solve(1)
    left, right = wait_back(1)
    one_out[...] = jnp.ones((N, LANES), F32)
    for k in range(N):
        value = part[1, k] + from_left[1, k] * left + from_right[1, k] * right
        t_out[across(k), :] = value[0]
        h_out[across(k), :] = value[1]

    for n in range(2):
        z_copy[n].wait_send()
    for _ in range(2 * SOLVERS):
        wait_slots(extra_send, 1, extra_sem.at[0])
    pull_copy.wait_send()
    pl.when(gy < N - 1)(y_up.wait_send)
    pl.when(gy > 0)(y_down.wait_send)
    for d in range(2):
        sent_to_solvers(d, coef_send, 0)
        sent_to_solvers(d, side_send, 1)
        pl.when(axes[d]["solves"])(
            lambda d=d: wait_slots(back_send.at[d], len(axes[d]["served"]), net_sem.at[d, 2, 0])
        )


def body(*args):
    flat = [a.reshape(N * N, LANES) for a in args]
    block = (N * N, LANES)
    rows = (N, 2, N, LANES)
    both = (2, N, 2, N, LANES)
    vmem = lambda *shape: pltpu.VMEM(shape, F32)
    outs = pl.pallas_call(
        kernel,
        out_shape=[jax.ShapeDtypeStruct(block, F32)] * 2 + [jax.ShapeDtypeStruct((N, LANES), F32)],
        in_specs=[pl.BlockSpec(memory_space=pltpu.HBM)] * 8,
        out_specs=[pl.BlockSpec(memory_space=pltpu.VMEM)] * 3,
        scratch_shapes=[
            vmem(2, *block),
            *[vmem(*block)] * 6,
            vmem(2, *block), vmem(*rows), vmem(2, *block),
            *[vmem(*both)] * 8,
            vmem(*rows), vmem(*rows),
            vmem(2, 2, N, LANES), vmem(2, 2, N, LANES),
            vmem(2, N, LANES), vmem(2, N, LANES),
            vmem(2, N, LANES), vmem(2, N, LANES),
            vmem(1, 1, LANES), vmem(N, 1, LANES),
            vmem(2, SOLVERS, 4, 8, LANES), vmem(2, N, 4, 8, LANES),
            vmem(2, SOLVERS, 2, 8, LANES), vmem(2, N, 2, 8, LANES),
            vmem(2, N, 2, 8, LANES), vmem(2, SOLVERS, 2, 8, LANES),
            vmem(2, N, 6, 8, LANES),
            pltpu.SemaphoreType.DMA((8,)),
            pltpu.SemaphoreType.DMA((2, 2)), pltpu.SemaphoreType.DMA((2, 2)),
            pltpu.SemaphoreType.DMA((2, 3, 2)), pltpu.SemaphoreType.DMA((2,)),
            pltpu.SemaphoreType.DMA((2,)), pltpu.SemaphoreType.REGULAR((3,)),
        ],
        compiler_params=pltpu.CompilerParams(
            collective_id=0, has_side_effects=True, vmem_limit_bytes=56229888
        ),
    )(*flat)
    return tuple(o.reshape(N, N, LANES) * outs[2][None] for o in outs[:2])


def solution(mesh):
    spec = P("gx", "gy", "gz")
    return jax.shard_map(
        body, mesh=mesh, in_specs=(spec,) * 8, out_specs=(spec,) * 2, check_vma=False
    )
```

```python
import functools

import jax
import jax.numpy as jnp
from jax import lax
from jax.experimental import pallas as pl
from jax.experimental.pallas import tpu as pltpu
from jax.sharding import PartitionSpec as P

vapour_scaling = 0.8
N = 16
LANES = 128
SOLVERS = 4
MESH = pl.DeviceIdType.MESH
F32 = jnp.float32


def kernel(
    t_in, h_in, load_in, k_in, kz_in, cx_in, cy_in, cz_in,
    t_out, h_out, one_out,
    fields, load, mix, mix_z, cfl_x, cfl_y, cfl_z,
    side, mask_z, half,
    first_w, last_w, inv, wi, ratio_c, from_left, from_right, part,
    tmp_a, tmp_b,
    y_send, y_face, z_send, z_face, pull_send, pull, extra_send, extra,
    coef_send, coef_recv, side_send, side_recv, back_send, back_recv, lu,
    in_sem, y_sem, z_sem, net_sem, pull_sem, extra_sem, far_sem,
):
    gx, gy, gz = lax.axis_index("gx"), lax.axis_index("gy"), lax.axis_index("gz")
    core = lax.rem(gx, 2)

    half_x, chip_x = lax.div(gx, N // 2), lax.rem(lax.div(gx, 2), 4)
    odd = lax.rem(gy + core, 2)

    def solver_x(other_half, step, other_core):
        c = lax.rem(core + other_core, 2)
        j = N // 2 * lax.rem(half_x + other_half, 2) + 2 * lax.rem(chip_x + step, 4) + c
        return lax.rem(j, 4), j

    def solver_y(step):
        j = lax.rem(gy + step - odd + N, N)
        return lax.rem(lax.div(j, 2), 4), j

    axes = (
        dict(
            me=gx, tile=lax.rem(gx, 4), solves=gx >= 0, device=lambda i: (i, gy, gz),
            solvers=[
                solver_x(*step, c)
                for step in ((1, 2), (1, 1), (1, 3), (0, 2), (1, 0), (0, 1), (0, 3), (0, 0)) for c in (1, 0)
            ],
            served=[4 * lax.div(gx, 4) + lax.rem(gx + step, 4) for step in (2, 3, 1)],
        ),
        dict(
            me=gy, tile=lax.rem(lax.div(gy, 2), 4), solves=odd == 0, device=lambda i: (gx, i, gz),
            solvers=[solver_y(step) for step in (8, -6, 6, -4, 4, -2, 2, 0)],
            served=[lax.rem(gy + step + N, N) for step in (4, -3, 3, -2, 2, -1, 1)],
        ),
    )

    loads = [
        pltpu.make_async_copy(src, dst, in_sem.at[n])
        for n, (src, dst) in enumerate((
            (k_in, mix), (cx_in, cfl_x), (t_in, fields.at[0]), (h_in, fields.at[1]),
            (cy_in, cfl_y), (kz_in, mix_z), (cz_in, cfl_z), (load_in, load),
        ))
    ]
    for copy in loads:
        copy.start()

    def ring(step):
        return (gx, lax.rem(gy + step + N, N), gz)

    def signal(sem, device):
        pl.semaphore_signal(sem, inc=1, device_id=device, device_id_type=MESH)

    barrier = pltpu.get_barrier_semaphore()
    signal(barrier, (gx, gy, 1 - gz))
    for step in (1, -1, 2, -2):
        signal(barrier, ring(step))

    @pl.loop(1, N)
    def _(step):
        signal(barrier, axes[0]["device"](lax.rem(gx + step, N)))

    expected = 5 + N - 1

    def tell(r):
        signal(far_sem.at[r], ring(2 << r))
        signal(far_sem.at[r], ring(-(2 << r)))

    def hear(r):
        pl.semaphore_wait(far_sem.at[r], 2)

    lane = lax.broadcasted_iota(jnp.int32, (2, N, LANES), 2)
    field = lax.broadcasted_iota(jnp.int32, (2, N, LANES), 0)
    ratio = jnp.where(field == 0, 1.0, vapour_scaling).astype(F32)
    weight = jnp.where(field == 0, 1.0, 0.0).astype(F32)
    lane2 = lax.broadcasted_iota(jnp.int32, (N, LANES), 1)
    face = jnp.where(gz == 0, LANES - 1, 0)

    def along(n):
        return pl.ds(N * n, N)

    def across(n):
        return pl.ds(n, N, stride=N)

    def pair(ref, rows):
        return jnp.broadcast_to(ref[rows, :][None], (2, N, LANES))

    def pack_column(rows, y, packed):
        for f in range(2):
            n = 1 + N * f + y
            moved = pltpu.roll(rows[f], n + 1 - gz, 1)
            packed = jnp.where(lane2 == n, moved, packed)
        return packed

    def unpack_column(packed, y):
        return jnp.stack(
            [pltpu.roll(packed, LANES - 1 - (1 + N * f + y) + gz, 1) for f in range(2)]
        )

    def factor(d, rows, cfl):
        def bands(k):
            mixed = ratio * pair(mix, rows(k))
            speed = 0.5 * pair(cfl, rows(k))
            return mixed - speed, mixed + speed

        rest, chain = None, None
        for k in range(N):
            east, west = bands(k)
            v = 1.0 + (west if rest is None else west * rest)
            i = 1.0 / (v + east)
            c = east * i
            rest = v * i
            w = west * i
            chain = w if chain is None else w * chain
            inv[d, k] = i
            wi[d, k] = w
            ratio_c[d, k] = c
            tmp_a[k] = chain
        q, t, prod = chain, c, None
        from_left[d, N - 1] = q
        from_right[d, N - 1] = t
        ends = [None, None, q, t]
        for k in range(N - 1, -1, -1):
            if k < N - 1:
                c = ratio_c[d, k]
                q = tmp_a[k] + c * q
                t = c * t
                from_left[d, k] = q
                from_right[d, k] = t
        ends[0], ends[1] = q, t
        for v, value in enumerate(ends):
            for s in range(SOLVERS):
                coef_send[d, s, v] = value[s // 2, 8 * (s % 2) : 8 * (s % 2) + 8]

    def weights(d, rows, cfl):
        def bands(k):
            mixed = ratio * pair(mix, rows(k))
            speed = 0.5 * pair(cfl, rows(k))
            return mixed - speed, mixed + speed

        rest, prod = None, None
        for k in range(N - 1, -1, -1):
            east, west = bands(k)
            v = 1.0 + (east if rest is None else east * rest)
            i = 1.0 / (v + west)
            rest = v * i
            tmp_a[k] = i
            tmp_b[k] = east * i
            last_w[d, k] = inv[d, k] if prod is None else inv[d, k] * prod
            prod = wi[d, k] if prod is None else wi[d, k] * prod
        prod = None
        for k in range(N):
            first_w[d, k] = tmp_a[k] if prod is None else tmp_a[k] * prod
            prod = tmp_b[k] if prod is None else tmp_b[k] * prod

    def to_solvers(d, send, recv, kind):
        ax = axes[d]
        for s, solver in ax["solvers"]:
            copy = pltpu.make_async_remote_copy(
                send.at[d, s], recv.at[d, ax["me"]],
                net_sem.at[d, kind, 0], net_sem.at[d, kind, 1],
                device_id=ax["device"](solver), device_id_type=MESH,
            )
            pl.when(ax["me"] != solver)(copy.start)

        @pl.when(ax["solves"])
        def _():
            recv[d, ax["me"]] = send[d, ax["tile"]]

    def wait_slots(ref, count, sem):
        pltpu.make_async_copy(ref.at[pl.ds(0, count)], ref.at[pl.ds(0, count)], sem).wait()

    def sent_to_solvers(d, send, kind):
        for _ in range(len(axes[d]["solvers"]) // SOLVERS - 1):
            wait_slots(send.at[d], SOLVERS, net_sem.at[d, kind, 0])
        pl.when(axes[d]["solves"])(
            lambda: wait_slots(send.at[d], SOLVERS - 1, net_sem.at[d, kind, 0])
        )
        pl.when(jnp.logical_not(axes[d]["solves"]))(
            lambda: wait_slots(send.at[d], SOLVERS, net_sem.at[d, kind, 0])
        )

    def solver_factor(d):
        @pl.when(axes[d]["solves"])
        def _():
            wait_slots(coef_recv.at[d], N - 1, net_sem.at[d, 0, 1])
            beta = None
            for i in range(N):
                q0, t0, q1, t1 = (coef_recv[d, i, v] for v in range(4))
                if beta is None:
                    dinv = jnp.ones_like(q0)
                    b = jnp.zeros_like(q0)
                    tau = t0
                    beta = t1
                    a = b
                    dq = b
                else:
                    dinv = 1.0 / (1.0 - q0 * beta)
                    b = q1 * beta * dinv
                    tau = t0 * dinv
                    beta = t1 + b * t0
                    a = q1 + b * q0
                    dq = dinv * q0
                for n, value in enumerate((dinv, dq, a, b, tau, beta)):
                    lu[d, i, n] = value

    def solver_solve(d):
        ax = axes[d]

        @pl.when(ax["solves"])
        def _():
            wait_slots(side_recv.at[d], N - 1, net_sem.at[d, 1, 1])
            if d == 1:
                wait_slots(extra, N, extra_sem.at[1])
            on_face = lane2[:8] == face
            start = 2 * N * lax.div(ax["tile"], 2) + 8 * lax.rem(ax["tile"], 2)
            spot = lane2[:8] - start - lax.broadcasted_iota(jnp.int32, (8, LANES), 0)
            alpha, alphas, phis = None, [], []
            for i in range(N):
                p0, p1 = side_recv[d, i, 0], side_recv[d, i, 1]
                if d == 1:
                    sent = jnp.broadcast_to(extra[i], (8, LANES))
                    d0, d1 = (
                        jnp.sum(jnp.where(spot == N * v, sent, 0.0), axis=1, keepdims=True) for v in range(2)
                    )
                    p0 = p0 + jnp.where(on_face, d0, 0.0)
                    p1 = p1 + jnp.where(on_face, d1, 0.0)
                if alpha is None:
                    phi, alpha = p0, p1
                else:
                    phi = lu[d, i, 0] * p0 + lu[d, i, 1] * alpha
                    alpha = (p1 + lu[d, i, 3] * p0) + lu[d, i, 2] * alpha
                alphas.append(alpha)
                phis.append(phi)
            zero = jnp.zeros((8, LANES), F32)
            first, firsts, lasts = zero, [None] * N, [None] * N
            for i in range(N - 1, -1, -1):
                lasts[i] = alphas[i] + lu[d, i, 5] * first
                first = phis[i] + lu[d, i, 4] * first
                firsts[i] = first
            for i in range(N):
                back_send[d, i, 0] = lasts[i - 1] if i > 0 else zero
                back_send[d, i, 1] = firsts[i + 1] if i < N - 1 else zero

            for j in ax["served"]:
                pltpu.make_async_remote_copy(
                    back_send.at[d, j], back_recv.at[d, ax["tile"]],
                    net_sem.at[d, 2, 0], net_sem.at[d, 2, 1],
                    device_id=ax["device"](j), device_id_type=MESH,
                ).start()

            back_recv[d, ax["tile"]] = back_send[d, ax["me"]]

    def wait_back(d):
        pl.when(axes[d]["solves"])(
            lambda: wait_slots(back_recv.at[d], SOLVERS - 1, net_sem.at[d, 2, 1])
        )
        pl.when(jnp.logical_not(axes[d]["solves"]))(
            lambda: wait_slots(back_recv.at[d], SOLVERS, net_sem.at[d, 2, 1])
        )
        return tuple(
            back_recv[d, :, v].reshape(2, N, LANES) for v in range(2)
        )

    def ends_of(d, rhs):
        sums = [None, None]
        for k in range(N):
            b = rhs(k)
            terms = first_w[d, k] * b, last_w[d, k] * b
            sums = [x if s is None else s + x for s, x in zip(sums, terms)]
        for v in range(2):
            for s in range(SOLVERS):
                side_send[d, s, v] = sums[v][s // 2, 8 * (s % 2) : 8 * (s % 2) + 8]

    def particular(d, rhs):
        g = None
        for k in range(N):
            g = inv[d, k] * rhs(k) + (0.0 if g is None else wi[d, k] * g)
            tmp_a[k] = g
        value = g
        part[d, N - 1] = value
        for k in range(N - 2, -1, -1):
            value = tmp_a[k] + ratio_c[d, k] * value
            part[d, k] = value

    loads[0].wait()
    loads[1].wait()
    factor(0, along, cfl_x)

    loads[2].wait()
    loads[3].wait()
    y_send[0] = fields[:, across(0), :]
    y_send[1] = fields[:, across(N - 1), :]
    packed = jnp.zeros((N, LANES), F32)
    for y in range(N):
        packed = pack_column(fields[:, across(y), :], y, packed)
    z_send[0] = packed
    pl.when(gy == 0)(lambda: y_face.__setitem__(0, jnp.zeros((2, N, LANES), F32)))
    pl.when(gy == N - 1)(lambda: y_face.__setitem__(1, jnp.zeros((2, N, LANES), F32)))

    pl.semaphore_wait(barrier, expected)

    z_copy = [
        pltpu.make_async_remote_copy(
            z_send.at[n], z_face.at[n], z_sem.at[n, 0], z_sem.at[n, 1],
            device_id=(gx, gy, 1 - gz), device_id_type=MESH,
        )
        for n in range(2)
    ]
    y_up = pltpu.make_async_remote_copy(
        y_send.at[1], y_face.at[0], y_sem.at[0, 0], y_sem.at[0, 1],
        device_id=(gx, gy + 1, gz), device_id_type=MESH,
    )
    y_down = pltpu.make_async_remote_copy(
        y_send.at[0], y_face.at[1], y_sem.at[1, 0], y_sem.at[1, 1],
        device_id=(gx, gy - 1, gz), device_id_type=MESH,
    )
    z_copy[0].start()
    pl.when(gy < N - 1)(y_up.start)
    pl.when(gy > 0)(y_down.start)
    tell(0)

    weights(0, along, cfl_x)

    for n in range(4, 8):
        loads[n].wait()
    toward = jnp.where(gz == 0, -0.5, 0.5).astype(F32)

    def vertical(v, y):
        mixed = ratio * pair(mix_z, across(y))
        cfl = pair(cfl_z, across(y))
        up = jnp.where(lane == LANES - 1, 0.0, pltpu.roll(v, LANES - 1, 2))
        down = jnp.where(lane == 0, 0.0, pltpu.roll(v, 1, 2))
        return (mixed - 0.5 * cfl) * (up - v) + (mixed + 0.5 * cfl) * (down - v)

    edge_coef = [None, None]
    for y in range(N):
        here = fields[:, across(y), :]
        mixed = ratio * pair(mix, across(y))
        speed = 0.5 * pair(cfl_y, across(y))
        east, west = mixed - speed, mixed + speed
        ahead = fields[:, across(y + 1), :] - here if y < N - 1 else -here
        behind = fields[:, across(y - 1), :] - here if y > 0 else -here
        value = here + (east * ahead + west * behind) + vertical(here, y)
        value = value + weight * pair(load, across(y))
        side[:, along(y), :] = value
        outward = ratio * pair(mix_z, across(y)) + toward * pair(cfl_z, across(y))
        mask_z[y] = jnp.where(lane == face, outward, 0.0)
        if y == 0:
            edge_coef[0] = west
        if y == N - 1:
            edge_coef[1] = east

    to_solvers(0, coef_send, coef_recv, 0)

    factor(1, across, cfl_y)
    weights(1, across, cfl_y)

    for v, ws in enumerate((first_w, last_w)):
        packed = jnp.zeros((N, LANES), F32)
        for y in range(N):
            packed = pack_column(ws[1, y] * mask_z[y], y, packed)
        pull_send[v] = packed
    pull_copy = pltpu.make_async_remote_copy(
        pull_send, pull, pull_sem.at[0], pull_sem.at[1],
        device_id=(gx, gy, 1 - gz), device_id_type=MESH,
    )
    pull_copy.start()
    hear(0)
    tell(1)

    z_copy[0].wait_recv()
    pl.when(gy > 0)(y_up.wait_recv)
    pl.when(gy < N - 1)(y_down.wait_recv)
    got = z_face[0]
    for y in range(N):
        value = side[:, along(y), :] + mask_z[y] * unpack_column(got, y)
        if y == 0:
            value = value + edge_coef[0] * y_face[0]
        if y == N - 1:
            value = value + edge_coef[1] * y_face[1]
        side[:, along(y), :] = value

    def first_rhs(k):
        return side[:, across(k), :]

    ends_of(0, first_rhs)
    to_solvers(0, side_send, side_recv, 1)
    solver_factor(0)
    hear(1)
    signal(far_sem.at[2], (gx, gy, 1 - gz))
    to_solvers(1, coef_send, coef_recv, 0)
    solver_solve(0)
    particular(0, first_rhs)
    left, right = wait_back(0)
    for k in range(N):
        half[:, along(k), :] = part[0, k] + from_left[0, k] * left + from_right[0, k] * right

    packed = jnp.zeros((N, LANES), F32)
    for y in range(N):
        packed = pack_column(half[:, across(y), :], y, packed)
    z_send[1] = packed
    z_copy[1].start()

    pull_copy.wait_recv()
    sums = [pull[v] * packed for v in range(2)]
    row = lax.broadcasted_iota(jnp.int32, (N, LANES), 0)
    spread = jnp.zeros((N, LANES), F32)
    for f in range(2):
        mine = jnp.logical_and(lane2 > N * f, lane2 <= N * f + N)
        for v in range(2):
            total = jnp.sum(jnp.where(mine, sums[v], 0.0), axis=1, keepdims=True)
            spread = jnp.where(lane2 == N * (2 * f + v) + row, total, spread)
    extra_send[0] = jnp.sum(spread, axis=0, keepdims=True)
    pl.semaphore_wait(far_sem.at[2], 1)
    for _, solver in axes[1]["solvers"]:
        pltpu.make_async_remote_copy(
            extra_send.at[0], extra.at[gy], extra_sem.at[0], extra_sem.at[1],
            device_id=(gx, solver, 1 - gz), device_id_type=MESH,
        ).start()

    for y in range(N):
        here = half[:, across(y), :]
        value = 2.0 * here - side[:, along(y), :] + vertical(here, y)
        side[:, along(y), :] = value + weight * pair(load, across(y))

    def second_rhs(k):
        return side[:, along(k), :]

    ends_of(1, second_rhs)
    to_solvers(1, side_send, side_recv, 1)
    z_copy[1].wait_recv()
    got = z_face[1]
    for y in range(N):
        side[:, along(y), :] = side[:, along(y), :] + mask_z[y] * unpack_column(got, y)
    particular(1, second_rhs)
    solver_factor(1)
    solver_solve(1)
    left, right = wait_back(1)
    one_out[...] = jnp.ones((N, LANES), F32)
    for k in range(N):
        value = part[1, k] + from_left[1, k] * left + from_right[1, k] * right
        t_out[across(k), :] = value[0]
        h_out[across(k), :] = value[1]

    for n in range(2):
        z_copy[n].wait_send()
    for _ in range(2 * SOLVERS):
        wait_slots(extra_send, 1, extra_sem.at[0])
    pull_copy.wait_send()
    pl.when(gy < N - 1)(y_up.wait_send)
    pl.when(gy > 0)(y_down.wait_send)
    for d in range(2):
        sent_to_solvers(d, coef_send, 0)
        sent_to_solvers(d, side_send, 1)
        pl.when(axes[d]["solves"])(
            lambda d=d: wait_slots(back_send.at[d], len(axes[d]["served"]), net_sem.at[d, 2, 0])
        )


def body(*args):
    flat = [a.reshape(N * N, LANES) for a in args]
    block = (N * N, LANES)
    rows = (N, 2, N, LANES)
    both = (2, N, 2, N, LANES)
    vmem = lambda *shape: pltpu.VMEM(shape, F32)
    outs = pl.pallas_call(
        kernel,
        out_shape=[jax.ShapeDtypeStruct(block, F32)] * 2 + [jax.ShapeDtypeStruct((N, LANES), F32)],
        in_specs=[pl.BlockSpec(memory_space=pltpu.HBM)] * 8,
        out_specs=[pl.BlockSpec(memory_space=pltpu.VMEM)] * 3,
        scratch_shapes=[
            vmem(2, *block),
            *[vmem(*block)] * 6,
            vmem(2, *block), vmem(*rows), vmem(2, *block),
            *[vmem(*both)] * 8,
            vmem(*rows), vmem(*rows),
            vmem(2, 2, N, LANES), vmem(2, 2, N, LANES),
            vmem(2, N, LANES), vmem(2, N, LANES),
            vmem(2, N, LANES), vmem(2, N, LANES),
            vmem(1, 1, LANES), vmem(N, 1, LANES),
            vmem(2, SOLVERS, 4, 8, LANES), vmem(2, N, 4, 8, LANES),
            vmem(2, SOLVERS, 2, 8, LANES), vmem(2, N, 2, 8, LANES),
            vmem(2, N, 2, 8, LANES), vmem(2, SOLVERS, 2, 8, LANES),
            vmem(2, N, 6, 8, LANES),
            pltpu.SemaphoreType.DMA((8,)),
            pltpu.SemaphoreType.DMA((2, 2)), pltpu.SemaphoreType.DMA((2, 2)),
            pltpu.SemaphoreType.DMA((2, 3, 2)), pltpu.SemaphoreType.DMA((2,)),
            pltpu.SemaphoreType.DMA((2,)), pltpu.SemaphoreType.REGULAR((3,)),
        ],
        compiler_params=pltpu.CompilerParams(
            collective_id=0, has_side_effects=True, vmem_limit_bytes=56229888
        ),
    )(*flat)
    return tuple(o.reshape(N, N, LANES) * outs[2][None] for o in outs[:2])


def solution(mesh):
    spec = P("gx", "gy", "gz")
    return jax.shard_map(
        body, mesh=mesh, in_specs=(spec,) * 8, out_specs=(spec,) * 2, check_vma=False
    )
```
